32 devices in a mesh: batch: 8 (over z, x), hidden: 4 (over y, core).
Axes of the slice: x: 2, y: 2, z: 4, core: 2. Of those that a mesh axis runs over, the one named last changes fastest.
Arguments:
- tokens: bfloat16 [5120, 4096], P('batch', 'hidden'), may hold values from -18 to 18
- segments: int32 [8, 640], P('batch'), may hold values from 0 to 5, never falling along the last dimension, each value on 1 to 256 neighbouring positions
- rel_bias: float32 [32, 64], P(None, 'hidden'), may hold values from -4 to 4
- ln_gain: float32 [4096], replicated, may hold values from 0.25 to 1.75
- w_query: bfloat16 [4096, 4096], P('batch', 'hidden'), may hold values from -0.04 to 0.04
- w_key: bfloat16 [4096, 4096], P('batch', 'hidden'), may hold values from -1 to 1
- w_value: bfloat16 [4096, 4096], P('batch', 'hidden'), may hold values from -0.09375 to 0.09375
- w_out: bfloat16 [4096, 4096], P('hidden', 'batch'), may hold values from -0.09375 to 0.09375
Outputs:
- output: bfloat16 [5120, 4096], P('batch', 'hidden')
The draws below stay inside these ranges and needn't reach their ends.
Inputs may be any that keep to these rules, and one draw needn't show every extreme that they name: `segments`: in each row (the 640 tokens of one group) passage ids start at 0 and grow by one at each new passage; every passage has 1 to 256 tokens, one has exactly 256, and all 6 ids occur.
All inputs are finite; a program needn't handle non-finite values.
Results may differ from the reference program's by a relative error of at most 0.0098.
Values may be sent and summed in bfloat16 or wider, within the bound.
No kernel may reach another device: no remote copies, remote signals or barrier semaphores. Data moves between devices by JAX's collectives and lax.ppermute only.
A program may use at most 128 MiB of HBM per device.

```python
import math
import jax
import jax.numpy as jnp
import numpy as np
from jax import lax

D = 4096
HEADS = 64
NUM_BUCKETS = 32
TOK_DEV = 640
PASSAGE = 256
INNER = 4096
QBLOCK = 640
KWIN = 640
SEGS = 6
GROUPS = 8
TOKENS = 5120
N_HIDDEN = 4


def query_entries(key):
    entry_key = jax.random.fold_in(key, 7102)
    entries = jnp.clip(jax.random.normal(entry_key, (D, INNER), jnp.float32), -6.0, 6.0)
    return entries * (1.0 / math.sqrt(8.0 * D))


def draw_w_query(key, part):
    return query_entries(key).astype(jnp.bfloat16)


def draw_w_key(key, part):
    own_key = jax.random.fold_in(key, 7103)
    entries = jnp.clip(jax.random.normal(own_key, (D, INNER), jnp.float32), -6.0, 6.0) * (1.0 / math.sqrt(D))
    return entries.astype(jnp.bfloat16)


def draw_tokens(key, part):
    first_key = jax.random.fold_in(jax.random.fold_in(key, 7201), 0)
    return jax.random.normal(first_key, (TOKENS, D), jnp.float32).astype(jnp.bfloat16)


def steps_of(key, extent, pieces, least, top_value):
    def one(position, parts):
        draws = jax.random.uniform(jax.random.fold_in(jax.random.fold_in(key, 6), position), (parts,), jnp.float32, least / len(pieces), top_value / len(pieces))
        return jnp.repeat(jnp.exp(draws), extent[position] // parts).reshape((-1,) + (1,) * (len(extent) - position - 1))

    gain = one(*pieces[0])
    for cut in pieces[1:]:
        gain = gain * one(*cut)
    return gain


def profile(count, total, limit, skew):
    loads = [(1 << 20) // math.isqrt(grade ** skew) + 1 for grade in range(2, count + 1)]
    rest, given = total - limit - (count - 1), [1] * (count - 1)
    while rest > 0:
        movable = [i for i in range(count - 1) if given[i] < limit]
        whole, budget = sum([loads[i] for i in movable]), rest
        for i in movable:
            addition = min(limit - given[i], max(1, budget * loads[i] // whole), rest)
            given[i] = given[i] + addition
            rest = rest - addition
    return np.array([limit] + given)


def ragged_sizes(key, amount, total, bound, skew):
    if amount == 2:
        one = jax.random.randint(key, (), max(1, total - bound), min(bound, total - 1) + 1)
        return jnp.stack([one, total - one])
    lengths = jnp.asarray(profile(amount, total, bound, skew), jnp.int32)
    pairs = (amount - 1) // 2
    donor, sink = lengths[1:1 + 2 * pairs:2], lengths[2:2 + 2 * pairs:2]
    slack = jnp.minimum(donor - 1, bound - sink)
    shifted = jax.random.randint(jax.random.fold_in(key, 1), (pairs,), 0, 1 << 20) % (slack + 1)
    lengths = lengths.at[1:1 + 2 * pairs:2].set(donor - shifted).at[2:2 + 2 * pairs:2].set(sink + shifted)
    return lengths[jax.random.permutation(jax.random.fold_in(key, 2), amount)]


def centred(rng, extent, scale, bound, cuts=(), kind=jnp.bfloat16):
    values = scale * jax.random.normal(rng, extent, jnp.float32)
    if cuts:
        values = values * steps_of(rng, extent, cuts, -0.22, 0.18)
    return jnp.clip(values, -bound, bound).astype(kind)


def setup_inputs(seed: int = 0) -> dict:
    streams_of = jax.random.split(jax.random.key(seed), 9)
    return {
        "tokens": draw_tokens(jax.random.fold_in(streams_of[8], 71), 0),
        "segments": jax.vmap(lambda own: jnp.searchsorted(jnp.cumsum(ragged_sizes(own, SEGS, TOK_DEV, PASSAGE, 1)), jnp.arange(TOK_DEV), side="right"))(jax.random.split(streams_of[1], GROUPS)).reshape((GROUPS, TOK_DEV)).astype(jnp.int32),
        "rel_bias": centred(streams_of[2], (NUM_BUCKETS, HEADS), 1.0, 4.0, ((1, 4),), jnp.float32),
        "ln_gain": jnp.clip(1.0 + 0.15 * jax.random.normal(streams_of[3], (D,), jnp.float32), 0.25, 1.75),
        "w_query": draw_w_query(jax.random.fold_in(streams_of[8], 71), 0),
        "w_key": draw_w_key(jax.random.fold_in(streams_of[8], 71), 0),
        "w_value": centred(streams_of[6], (D, INNER), D ** -0.5, 0.09375, ((0, 8), (1, 4))),
        "w_out": centred(streams_of[7], (INNER, D), INNER ** -0.5, 0.09375, ((0, 4), (1, 8))),
    }


norm_epsilon = 1e-06
bucket_edges = (12, 16, 23, 32, 46, 64, 91)
masked_score = -1e+30

def bucket_of(offsets):
    distance = jnp.abs(offsets)
    reached = sum(((distance >= threshold).astype(jnp.int32) for threshold in bucket_edges))
    within = jnp.where(distance < 8, distance, 8 + reached)
    return (within + jnp.where(offsets > 0, 16, 0)).astype(jnp.int32)

def attend_group(queries, keys_here, values_here, passage, bias_table):
    length_here = queries.shape[0]
    heads_here = bias_table.shape[1]
    head_width = queries.shape[1] // heads_here
    relative = (jnp.arange(KWIN, dtype=jnp.int32)[None, :] - jnp.arange(QBLOCK, dtype=jnp.int32)[:, None]).astype(jnp.int32)

    def one_block(first_row):
        window_start = jnp.clip(first_row - PASSAGE, 0, length_here - KWIN).astype(jnp.int32)
        query_block = lax.dynamic_slice_in_dim(queries, first_row, QBLOCK, 0).reshape(QBLOCK, heads_here, head_width)
        key_block = lax.dynamic_slice_in_dim(keys_here, window_start, KWIN, 0).reshape(KWIN, heads_here, head_width)
        value_block = lax.dynamic_slice_in_dim(values_here, window_start, KWIN, 0).reshape(KWIN, heads_here, head_width)
        scores = jnp.einsum('qhd,khd->hqk', query_block.astype(jnp.float32), key_block.astype(jnp.float32))
        buckets = bucket_of(window_start - first_row + relative)
        position_bias = jnp.transpose(jnp.take(bias_table, buckets, axis=0), (2, 0, 1))
        query_ids = lax.dynamic_slice_in_dim(passage, first_row, QBLOCK, 0)
        key_ids = lax.dynamic_slice_in_dim(passage, window_start, KWIN, 0)
        same_passage = query_ids[:, None] == key_ids[None, :]
        scores = jnp.where(same_passage[None], scores + position_bias, masked_score)
        row_max = lax.optimization_barrier(jnp.max(scores, axis=2, keepdims=True))
        raised = jnp.exp(scores - row_max)
        attention_weights = (raised / lax.optimization_barrier(jnp.sum(raised, axis=2, keepdims=True))).astype(jnp.bfloat16)
        combined = jnp.einsum('hqk,khd->qhd', attention_weights.astype(jnp.float32), value_block.astype(jnp.float32))
        return combined.astype(jnp.bfloat16).reshape(QBLOCK, heads_here * head_width)
    starts = jnp.arange(length_here // QBLOCK, dtype=jnp.int32) * QBLOCK
    blocks = lax.map(one_block, starts)
    return blocks.reshape(length_here, heads_here * head_width)

def reference(tokens, segments, rel_bias, ln_gain, w_query, w_key, w_value, w_out):
    residual = tokens.astype(jnp.float32)
    variance = lax.optimization_barrier(jnp.mean(residual * residual, axis=1, keepdims=True))
    normed = (residual * lax.rsqrt(variance + norm_epsilon) * ln_gain).astype(jnp.bfloat16)
    queries = jnp.dot(normed, w_query, preferred_element_type=jnp.float32).astype(jnp.bfloat16)
    keys_all = jnp.dot(normed, w_key, preferred_element_type=jnp.float32).astype(jnp.bfloat16)
    values_all = jnp.dot(normed, w_value, preferred_element_type=jnp.float32).astype(jnp.bfloat16)

    def one_group(operands):
        group_queries, group_keys, group_values, passage = operands
        return attend_group(group_queries, group_keys, group_values, passage, rel_bias)
    attended = lax.map(one_group, (queries.reshape(GROUPS, TOK_DEV, INNER), keys_all.reshape(GROUPS, TOK_DEV, INNER), values_all.reshape(GROUPS, TOK_DEV, INNER), segments))
    attended = attended.reshape(TOKENS, INNER)
    block_width = INNER // N_HIDDEN
    output = residual
    for portion_index in range(N_HIDDEN):
        lower_row = portion_index * block_width
        partial_product = jnp.dot(attended[:, lower_row:lower_row + block_width], w_out[lower_row:lower_row + block_width], preferred_element_type=jnp.float32)
        rounded = lax.optimization_barrier(partial_product.astype(jnp.bfloat16))
        output = output + rounded.astype(jnp.float32)
    return output.astype(jnp.bfloat16)
```

```python
import functools

import jax
import jax.numpy as jnp
from jax import lax
from jax.experimental import pallas as pl
from jax.experimental.pallas import tpu as pltpu
from jax.sharding import PartitionSpec as P

PASSAGE = 256
BLOCK = 128

norm_epsilon = 1e-06
bucket_edges = (12, 16, 23, 32, 46, 64, 91)
masked_score = -1e30


def bucket_of(offsets):
    distance = jnp.abs(offsets)
    reached = sum(((distance >= threshold).astype(jnp.int32) for threshold in bucket_edges))
    within = jnp.where(distance < 8, distance, 8 + reached)
    return within + jnp.where(offsets > 0, 16, 0)


def bias_tiles(table):
    rows = 2 * PASSAGE + BLOCK
    offsets = (
        jnp.arange(rows, dtype=jnp.int32)[:, None]
        - PASSAGE
        - jnp.arange(BLOCK, dtype=jnp.int32)[None, :]
    )
    buckets = bucket_of(offsets)[None]
    tiles = jnp.zeros((table.shape[1], rows, BLOCK), jnp.float32)
    for level in range(table.shape[0]):
        tiles = jnp.where(buckets == level, table[level][:, None, None], tiles)
    return tiles


def attention_kernel(width, q_ids, k_ids, bias, queries, keys, values, out):
    length = keys.shape[0]
    blocks = length // BLOCK
    reach = PASSAGE // BLOCK
    heads = keys.shape[1] // width
    for i in range(blocks):
        low, high = max(0, i - reach) * BLOCK, min(blocks, i + reach + 1) * BLOCK
        columns = slice(i * BLOCK, (i + 1) * BLOCK)
        first = low - i * BLOCK + PASSAGE
        same = k_ids[low:high, :] == q_ids[:, columns]
        for h in range(heads):
            rows = slice(h * width, (h + 1) * width)
            own = queries[rows, columns]
            blank = jnp.zeros_like(own)
            spread = jnp.concatenate([own if g == h else blank for g in range(heads)], axis=0)
            scores = jnp.dot(keys[low:high, :], spread, preferred_element_type=jnp.float32)
            scores = jnp.where(same, scores + bias[h, first : first + high - low, :], masked_score)
            raised = jnp.exp(scores - jnp.max(scores, axis=0, keepdims=True)).astype(jnp.bfloat16)
            extended = jnp.concatenate(
                [values[rows, low:high], jnp.ones((16, high - low), jnp.bfloat16)], axis=0
            )
            total = jnp.dot(extended, raised, preferred_element_type=jnp.float32)
            out[rows, columns] = (total[:width] / total[width : width + 1]).astype(jnp.bfloat16)


def attend(queries, keys, values, ids, bias, group, width):
    length = ids.shape[0]
    features = keys.shape[1]
    pair = 128 // width
    wide_ids = jnp.broadcast_to(ids[:, None], (length, BLOCK))
    return pl.pallas_call(
        functools.partial(attention_kernel, width),
        grid=(features // 128,),
        in_specs=[
            pl.BlockSpec((1, length), lambda p: (0, 0)),
            pl.BlockSpec((length, BLOCK), lambda p: (0, 0)),
            pl.BlockSpec((pair,) + bias.shape[1:], lambda p: (p, 0, 0)),
            pl.BlockSpec((128, length), lambda p: (p, group)),
            pl.BlockSpec((length, 128), lambda p: (group, p)),
            pl.BlockSpec((128, length), lambda p: (p, group)),
        ],
        out_specs=pl.BlockSpec((128, length), lambda p: (p, 0)),
        out_shape=jax.ShapeDtypeStruct((features, length), jnp.bfloat16),
        compiler_params=pltpu.CompilerParams(vmem_limit_bytes=24 * 1024 * 1024),
        cost_estimate=pl.CostEstimate(
            flops=8 * features * length * length,
            bytes_accessed=16 * features * length,
            transcendentals=features // width * length * length,
        ),
    )(ids[None, :], wide_ids, bias, queries, keys, values)


def after(value, earlier):
    return lax.optimization_barrier((value, earlier))[0]


def per_device(n_batch, n_hidden, tokens, segments, rel_bias, ln_gain, w_query, w_key, w_value, w_out):
    place = lax.axis_index("batch")
    column = lax.axis_index("hidden")
    parity = (place >> 1) & 1
    length, own_width = tokens.shape
    heads = rel_bias.shape[1] // 2
    half = w_query.shape[1] // 2
    width = half // heads

    def swap(value, step, axis="batch"):
        count = n_batch if axis == "batch" else n_hidden
        return lax.ppermute(value, axis, [(i, i ^ step) for i in range(count)])

    peer_tokens = swap(tokens, 2)
    peer_ids = swap(segments, 2)
    gathered = [
        lax.all_gather(part, "hidden", axis=1, tiled=True) for part in (tokens, peer_tokens)
    ]

    history_far, history_near = [peer_tokens, peer_tokens], []

    def paced(value, step, history):
        if len(history) >= 2:
            value = after(value, history[-2])
        received = swap(value, step)
        history.append(received)
        return received

    def collect(weight, axis):
        halves = [
            lax.dynamic_slice_in_dim(weight, side * (weight.shape[axis] // 2), weight.shape[axis] // 2, axis)
            for side in (parity, 1 - parity)
        ]
        pieces = {0: halves[0]}
        far = list(range(n_batch - 2, 0, -2))
        for step in far:
            pieces[step] = paced(halves[(step >> 1) & 1], step, history_far)
        for step in [0] + far:
            pieces[step ^ 1] = paced(pieces[step], 1, history_near)
        return pieces

    key_pieces = collect(w_key, 1)
    query_pieces = collect(w_query, 1)
    value_pieces = collect(w_value, 1)
    out_pieces = collect(w_out, 0)

    table = lax.dynamic_slice_in_dim(rel_bias, parity * heads, heads, 1)
    bias = bias_tiles(table)

    both = jnp.concatenate(gathered, axis=0).astype(jnp.float32)
    scale = lax.rsqrt(jnp.mean(both * both, axis=1, keepdims=True) + norm_epsilon)
    depth = w_query.shape[0]

    def normed_part(step):
        start = (place ^ step) * depth
        return (
            lax.dynamic_slice_in_dim(both, start, depth, 1)
            * scale
            * lax.dynamic_slice_in_dim(ln_gain, start, depth, 0)
        ).astype(jnp.bfloat16)

    order = [s for e in [0] + list(range(n_batch - 2, 0, -2)) for s in (e, e ^ 1)]
    rounds = [order[: n_batch // 2], order[n_batch // 2 :]]
    normed = [jnp.concatenate([normed_part(step) for step in steps], axis=1) for steps in rounds]

    def project(pieces, form):
        total = None
        for part, steps in zip(normed, rounds):
            rows = jnp.concatenate([pieces[step] for step in steps], axis=0)
            term = jnp.einsum(form, part, rows, preferred_element_type=jnp.float32)
            total = term if total is None else total + term
        return total.astype(jnp.bfloat16)

    keys = project(key_pieces, "td,df->tf")
    queries = project(query_pieces, "td,df->ft")
    values = project(value_pieces, "td,df->ft")

    out_width = w_out.shape[1]
    w_out_here = jnp.zeros((half, out_width * n_batch), jnp.bfloat16)
    for step in range(n_batch):
        w_out_here = lax.dynamic_update_slice_in_dim(
            w_out_here, out_pieces[step], (place ^ step) * out_width, 1
        )

    def partial_sums(attended):
        def block(step):
            rows = lax.dynamic_slice_in_dim(w_out_here, (column ^ step) * own_width, own_width, 1)
            return jnp.einsum("ft,fc->tc", attended, rows, preferred_element_type=jnp.float32)

        def rounded(value):
            return value.astype(jnp.bfloat16)

        far = swap(rounded(block(3)), 1, "hidden")
        near = swap(rounded(block(1)), 1, "hidden")
        across = swap(rounded(block(2) + far.astype(jnp.float32)), 2, "hidden")
        return block(0) + near.astype(jnp.float32) + across.astype(jnp.float32)

    peer = partial_sums(attend(queries, keys, values, peer_ids[0], bias, 1, width))
    from_peer = swap(peer.astype(jnp.bfloat16), 2)
    own = partial_sums(attend(queries, keys, values, segments[0], bias, 0, width))
    return (tokens.astype(jnp.float32) + own + from_peer.astype(jnp.float32)).astype(jnp.bfloat16)


def solution(mesh):
    placed = (
        P("batch", "hidden"),
        P("batch", None),
        P(None, "hidden"),
        P(),
        P("batch", "hidden"),
        P("batch", "hidden"),
        P("batch", "hidden"),
        P("hidden", "batch"),
    )
    return jax.shard_map(
        functools.partial(per_device, mesh.shape["batch"], mesh.shape["hidden"]),
        mesh=mesh,
        in_specs=placed,
        out_specs=P("batch", "hidden"),
        check_vma=False,
    )
```

```python
import functools

import jax
import jax.numpy as jnp
from jax import lax
from jax.experimental import pallas as pl
from jax.experimental.pallas import tpu as pltpu
from jax.sharding import PartitionSpec as P

PASSAGE = 256
BLOCK = 128

norm_epsilon = 1e-06
bucket_edges = (12, 16, 23, 32, 46, 64, 91)
masked_score = -1e30


def bucket_of(offsets):
    distance = jnp.abs(offsets)
    reached = sum(((distance >= threshold).astype(jnp.int32) for threshold in bucket_edges))
    within = jnp.where(distance < 8, distance, 8 + reached)
    return within + jnp.where(offsets > 0, 16, 0)


def bias_tiles(table):
    rows = 2 * PASSAGE + BLOCK
    offsets = (
        jnp.arange(rows, dtype=jnp.int32)[:, None]
        - PASSAGE
        - jnp.arange(BLOCK, dtype=jnp.int32)[None, :]
    )
    buckets = bucket_of(offsets)[None]
    tiles = jnp.zeros((table.shape[1], rows, BLOCK), jnp.float32)
    for level in range(table.shape[0]):
        tiles = jnp.where(buckets == level, table[level][:, None, None], tiles)
    return tiles


def attention_kernel(width, q_ids, k_ids, bias, queries, keys, values, out):
    length = keys.shape[0]
    blocks = length // BLOCK
    reach = PASSAGE // BLOCK
    heads = keys.shape[1] // width
    for i in range(blocks):
        low, high = max(0, i - reach) * BLOCK, min(blocks, i + reach + 1) * BLOCK
        columns = slice(i * BLOCK, (i + 1) * BLOCK)
        first = low - i * BLOCK + PASSAGE
        same = k_ids[low:high, :] == q_ids[:, columns]
        for h in range(heads):
            rows = slice(h * width, (h + 1) * width)
            own = queries[rows, columns]
            blank = jnp.zeros_like(own)
            spread = jnp.concatenate([own if g == h else blank for g in range(heads)], axis=0)
            scores = jnp.dot(keys[low:high, :], spread, preferred_element_type=jnp.float32)
            scores = jnp.where(same, scores + bias[h, first : first + high - low, :], masked_score)
            raised = jnp.exp(scores - jnp.max(scores, axis=0, keepdims=True)).astype(jnp.bfloat16)
            extended = jnp.concatenate(
                [values[rows, low:high], jnp.ones((16, high - low), jnp.bfloat16)], axis=0
            )
            total = jnp.dot(extended, raised, preferred_element_type=jnp.float32)
            out[rows, columns] = (total[:width] / total[width : width + 1]).astype(jnp.bfloat16)


def attend(queries, keys, values, ids, bias, group, width):
    length = ids.shape[0]
    features = keys.shape[1]
    pair = 128 // width
    wide_ids = jnp.broadcast_to(ids[:, None], (length, BLOCK))
    return pl.pallas_call(
        functools.partial(attention_kernel, width),
        grid=(features // 128,),
        in_specs=[
            pl.BlockSpec((1, length), lambda p: (0, 0)),
            pl.BlockSpec((length, BLOCK), lambda p: (0, 0)),
            pl.BlockSpec((pair,) + bias.shape[1:], lambda p: (p, 0, 0)),
            pl.BlockSpec((128, length), lambda p: (p, group)),
            pl.BlockSpec((length, 128), lambda p: (group, p)),
            pl.BlockSpec((128, length), lambda p: (p, group)),
        ],
        out_specs=pl.BlockSpec((128, length), lambda p: (p, 0)),
        out_shape=jax.ShapeDtypeStruct((features, length), jnp.bfloat16),
        compiler_params=pltpu.CompilerParams(vmem_limit_bytes=24 * 1024 * 1024),
        cost_estimate=pl.CostEstimate(
            flops=8 * features * length * length,
            bytes_accessed=16 * features * length,
            transcendentals=features // width * length * length,
        ),
    )(ids[None, :], wide_ids, bias, queries, keys, values)


def after(value, earlier):
    return lax.optimization_barrier((value, earlier))[0]


def per_device(n_batch, n_hidden, tokens, segments, rel_bias, ln_gain, w_query, w_key, w_value, w_out):
    place = lax.axis_index("batch")
    column = lax.axis_index("hidden")
    parity = (place >> 1) & 1
    length, own_width = tokens.shape
    heads = rel_bias.shape[1] // 2
    half = w_query.shape[1] // 2
    width = half // heads

    def swap(value, step, axis="batch"):
        count = n_batch if axis == "batch" else n_hidden
        return lax.ppermute(value, axis, [(i, i ^ step) for i in range(count)])

    def halves(weight, axis):
        size = weight.shape[axis] // 2
        return [
            lax.dynamic_slice_in_dim(weight, side * size, size, axis)
            for side in (parity, 1 - parity)
        ]

    far_steps = list(range(n_batch - 2, 2, -2))
    far_line, near_line = [], []

    def paced(value, step, line, *earlier):
        waits = tuple(line[-2:-1]) + earlier
        if waits:
            value = after(value, waits)
        received = swap(value, step)
        line.append(received)
        return received

    def along_z(parts, earlier):
        pieces = {0: parts[0]}
        for step in far_steps:
            pieces[step] = paced(parts[(step >> 1) & 1], step, far_line, *earlier.get(step, ()))
        pieces[2] = swap(after(parts[1], far_line[-2:-1]), 2)
        return pieces

    def along_x(pieces, steps, earlier):
        for step in steps:
            pieces[step ^ 1] = paced(pieces[step], 1, near_line, *earlier.get(step, ()))

    peer_tokens = swap(tokens, 2)
    peer_ids = swap(segments, 2)

    def all_features(part):
        across = swap(part, 2, "hidden")
        return [part, swap(part, 1, "hidden"), across, swap(across, 1, "hidden")]

    gathered = [all_features(part) for part in (tokens, peer_tokens)]

    key_pieces = along_z(halves(w_key, 1), {})
    query_parts = halves(w_query, 1)
    query_pieces = along_z(query_parts, {})
    value_parts = halves(w_value, 1)
    others = far_steps + [2]
    along_x(key_pieces, [0], {})
    along_x(query_pieces, [0], {})
    along_x(key_pieces, others, {})
    along_x(query_pieces, others, {})

    table = lax.dynamic_slice_in_dim(rel_bias, parity * heads, heads, 1)
    bias = bias_tiles(table)

    both = jnp.concatenate([jnp.concatenate(parts, axis=1) for parts in gathered], axis=0)
    wide = both.astype(jnp.float32)
    scale = lax.rsqrt(jnp.mean(wide * wide, axis=1, keepdims=True) + norm_epsilon)
    depth = w_query.shape[0]
    per_block = own_width // depth

    def normed_part(step):
        source = place ^ step
        where = ((source // per_block) ^ column) * own_width + (source % per_block) * depth
        return (
            lax.dynamic_slice_in_dim(both, where, depth, 1).astype(jnp.float32)
            * scale
            * lax.dynamic_slice_in_dim(ln_gain, source * depth, depth, 0)
        ).astype(jnp.bfloat16)

    order = [s for e in [0] + others for s in (e, e ^ 1)]
    rounds = [order[: n_batch // 2], order[n_batch // 2 :]]
    normed = [jnp.concatenate([normed_part(step) for step in steps], axis=1) for steps in rounds]

    def project(pieces, form):
        total = None
        for part, steps in zip(normed, rounds):
            rows = jnp.concatenate([pieces[step] for step in steps], axis=0)
            term = jnp.einsum(form, part, rows, preferred_element_type=jnp.float32)
            total = term if total is None else total + term
        return total.astype(jnp.bfloat16)

    keys = project(key_pieces, "td,df->tf")
    queries = project(query_pieces, "td,df->ft")
    last = far_steps[-1]
    value_pieces = along_z(value_parts, {last: (normed[0], normed[1])})
    along_x(value_pieces, [0] + others, {})
    values = project(value_pieces, "td,df->ft")

    out_pieces = along_z(halves(w_out, 0), {far_steps[0]: (keys,), last: (queries,)})
    along_x(out_pieces, [0], {})
    attended = [attend(queries, keys, values, peer_ids[0], bias, 1, width)]
    along_x(out_pieces, [2] + far_steps, {last: (attended[0],)})
    attended.insert(0, attend(queries, keys, values, segments[0], bias, 0, width))
    attended = jnp.concatenate(attended, axis=1)

    side = place & 1
    stripes = own_width // (2 * w_out.shape[1])

    def sums(parity_step):
        rows = jnp.concatenate([out_pieces[e ^ parity_step] for e in range(0, n_batch, 2)], axis=0)

        def block(step):
            first = (column ^ step) * stripes
            chosen = [
                lax.dynamic_slice_in_dim(rows, ((place >> 1) ^ (first + j)) * half, half, 0)
                for j in range(stripes)
            ]
            chosen = chosen[0] if stripes == 1 else jnp.concatenate(chosen, axis=1)
            return jnp.einsum("ft,fc->tc", attended, chosen, preferred_element_type=jnp.float32)

        far = send(block(3), 1, "hidden")
        near = send(block(1), 1, "hidden")
        return block(0) + near, block(2) + far

    def send(value, step, axis="batch"):
        return swap(value.astype(jnp.bfloat16), step, axis).astype(jnp.float32)

    here, there = sums(0)
    first = here + send(there, 2, "hidden")
    first = first[:length] + send(first[length:], 2)
    here, there = sums(1)
    there = there[:length] + send(there[length:], 2)
    second = here[:length] + send(here[length:], 2) + send(there, 2, "hidden")

    parts = [v.reshape(length, stripes, w_out.shape[1]) for v in (first, second)]
    combined = jnp.where(side == 0, jnp.stack(parts, 2), jnp.stack(parts[::-1], 2))
    return (tokens.astype(jnp.float32) + combined.reshape(length, own_width)).astype(jnp.bfloat16)


def solution(mesh):
    placed = (
        P("batch", "hidden"),
        P("batch", None),
        P(None, "hidden"),
        P(),
        P("batch", "hidden"),
        P("batch", "hidden"),
        P("batch", "hidden"),
        P("hidden", "batch"),
    )
    return jax.shard_map(
        functools.partial(per_device, mesh.shape["batch"], mesh.shape["hidden"]),
        mesh=mesh,
        in_specs=placed,
        out_specs=P("batch", "hidden"),
        check_vma=False,
    )
```

```python
import functools

import jax
import jax.numpy as jnp
from jax import lax
from jax.experimental import pallas as pl
from jax.experimental.pallas import tpu as pltpu
from jax.sharding import PartitionSpec as P

PASSAGE = 256
BLOCK = 128

norm_epsilon = 1e-06
bucket_edges = (12, 16, 23, 32, 46, 64, 91)
masked_score = -1e30


def bucket_of(offsets):
    distance = jnp.abs(offsets)
    reached = sum(((distance >= threshold).astype(jnp.int32) for threshold in bucket_edges))
    within = jnp.where(distance < 8, distance, 8 + reached)
    return within + jnp.where(offsets > 0, 16, 0)


def bias_tiles(table):
    rows = 2 * PASSAGE + BLOCK
    offsets = (
        jnp.arange(rows, dtype=jnp.int32)[:, None]
        - PASSAGE
        - jnp.arange(BLOCK, dtype=jnp.int32)[None, :]
    )
    buckets = bucket_of(offsets)[None]
    tiles = jnp.zeros((table.shape[1], rows, BLOCK), jnp.float32)
    for level in range(table.shape[0]):
        tiles = jnp.where(buckets == level, table[level][:, None, None], tiles)
    return tiles


def attention_kernel(width, q_ids, k_ids, bias, queries, keys, values, out):
    length = keys.shape[0]
    blocks = length // BLOCK
    reach = PASSAGE // BLOCK
    heads = keys.shape[1] // width
    for i in range(blocks):
        low, high = max(0, i - reach) * BLOCK, min(blocks, i + reach + 1) * BLOCK
        columns = slice(i * BLOCK, (i + 1) * BLOCK)
        first = low - i * BLOCK + PASSAGE
        same = k_ids[low:high, :] == q_ids[:, columns]
        for h in range(heads):
            rows = slice(h * width, (h + 1) * width)
            own = queries[rows, columns]
            blank = jnp.zeros_like(own)
            spread = jnp.concatenate([own if g == h else blank for g in range(heads)], axis=0)
            scores = jnp.dot(keys[low:high, :], spread, preferred_element_type=jnp.float32)
            scores = jnp.where(same, scores + bias[h, first : first + high - low, :], masked_score)
            raised = jnp.exp(scores - jnp.max(scores, axis=0, keepdims=True)).astype(jnp.bfloat16)
            extended = jnp.concatenate(
                [values[rows, low:high], jnp.ones((16, high - low), jnp.bfloat16)], axis=0
            )
            total = jnp.dot(extended, raised, preferred_element_type=jnp.float32)
            out[rows, columns] = (total[:width] / total[width : width + 1]).astype(jnp.bfloat16)


def attend(queries, keys, values, ids, bias, group, width):
    length = ids.shape[0]
    features = keys.shape[1]
    pair = 128 // width
    wide_ids = jnp.broadcast_to(ids[:, None], (length, BLOCK))
    return pl.pallas_call(
        functools.partial(attention_kernel, width),
        grid=(features // 128,),
        in_specs=[
            pl.BlockSpec((1, length), lambda p: (0, 0)),
            pl.BlockSpec((length, BLOCK), lambda p: (0, 0)),
            pl.BlockSpec((pair,) + bias.shape[1:], lambda p: (p, 0, 0)),
            pl.BlockSpec((128, length), lambda p: (p, group)),
            pl.BlockSpec((length, 128), lambda p: (group, p)),
            pl.BlockSpec((128, length), lambda p: (p, group)),
        ],
        out_specs=pl.BlockSpec((128, length), lambda p: (p, 0)),
        out_shape=jax.ShapeDtypeStruct((features, length), jnp.bfloat16),
        compiler_params=pltpu.CompilerParams(vmem_limit_bytes=24 * 1024 * 1024),
        cost_estimate=pl.CostEstimate(
            flops=8 * features * length * length,
            bytes_accessed=16 * features * length,
            transcendentals=features // width * length * length,
        ),
    )(ids[None, :], wide_ids, bias, queries, keys, values)


def after(value, earlier):
    return lax.optimization_barrier((value, earlier))[0]


def per_device(n_batch, n_hidden, tokens, segments, rel_bias, ln_gain, w_query, w_key, w_value, w_out):
    place = lax.axis_index("batch")
    column = lax.axis_index("hidden")
    parity = (place >> 1) & 1
    length, own_width = tokens.shape
    heads = rel_bias.shape[1] // 2
    half = w_query.shape[1] // 2
    width = half // heads

    def swap(value, step, axis="batch"):
        count = n_batch if axis == "batch" else n_hidden
        return lax.ppermute(value, axis, [(i, i ^ step) for i in range(count)])

    planes = n_batch // 4
    plane = place >> 2
    near_line = []

    def paired(weight, axis, *earlier):
        size = weight.shape[axis] // 2
        kept, given = [
            lax.dynamic_slice_in_dim(weight, side * size, size, axis)
            for side in (parity, 1 - parity)
        ]
        if earlier:
            given = after(given, earlier)
        return jnp.concatenate([kept, swap(given, 2)], axis=0)

    def along_z(pair):
        groups = [[r + 4 * i for i in range(planes)] for r in range(4)]
        return lax.all_gather(pair, "batch", axis=0, tiled=True, axis_index_groups=groups)

    def along_x(value, *earlier):
        waits = tuple(near_line[-2:-1]) + earlier
        if waits:
            value = after(value, waits)
        received = swap(value, 1)
        near_line.append(received)
        return received

    def others(whole):
        size = whole.shape[0] // planes
        rest = [
            lax.dynamic_slice_in_dim(whole, (plane ^ k) * size, size, 0) for k in range(1, planes)
        ]
        return rest[0] if len(rest) == 1 else jnp.concatenate(rest, axis=0)

    key_pair = paired(w_key, 1)

    peer_tokens = swap(tokens, 2)
    peer_ids = swap(segments, 2)
    across = jnp.concatenate([swap(tokens, 2, "hidden"), swap(peer_tokens, 2, "hidden")], axis=0)
    held = jnp.concatenate([jnp.concatenate([tokens, peer_tokens], axis=0), across], axis=1)
    other = swap(held, 1, "hidden")

    query_pair = paired(w_query, 1, key_pair)
    value_pair = paired(w_value, 1, query_pair)
    out_pair = paired(w_out, 0, value_pair)
    key_whole = along_z(key_pair)
    query_whole = along_z(after(query_pair, key_pair))
    value_whole = along_z(after(value_pair, query_pair))
    out_whole = along_z(after(out_pair, value_pair))

    key_near = along_x(key_pair)
    query_near = along_x(query_pair)
    key_rest = along_x(others(key_whole))
    value_near = along_x(value_pair)
    query_rest = along_x(others(query_whole))

    table = lax.dynamic_slice_in_dim(rel_bias, parity * heads, heads, 1)
    bias = bias_tiles(table)

    depth = w_query.shape[0]
    per_block = own_width // depth

    def squares(value):
        value = value.astype(jnp.float32)
        return jnp.sum(value * value, axis=1, keepdims=True)

    scale = lax.rsqrt((squares(held) + squares(other)) / (2 * held.shape[1]) + norm_epsilon)

    def normed_part(source):
        block = (source // per_block) ^ column
        where = (block >> 1) * own_width + (source % per_block) * depth
        chosen = jnp.where(
            (block & 1) == 0,
            lax.dynamic_slice_in_dim(held, where, depth, 1),
            lax.dynamic_slice_in_dim(other, where, depth, 1),
        )
        gain = lax.dynamic_slice_in_dim(ln_gain, source * depth, depth, 0)
        return (chosen.astype(jnp.float32) * scale * gain).astype(jnp.bfloat16)

    def normed_parts(sources):
        return jnp.concatenate([normed_part(source) for source in sources], axis=1)

    normed_near = normed_parts([place ^ (2 * j + 1) for j in range(2)])
    normed_whole = normed_parts(
        [4 * i + ((place & 3) ^ (2 * j)) for i in range(planes) for j in range(2)]
    )
    normed_rest = normed_parts(
        [place ^ (4 * k + 2 * j + 1) for k in range(1, planes) for j in range(2)]
    )

    def project(near, whole, rest, form):
        total = None
        for part, rows in ((normed_near, near), (normed_whole, whole), (normed_rest, rest)):
            term = jnp.einsum(form, part, rows, preferred_element_type=jnp.float32)
            total = term if total is None else total + term
        return total.astype(jnp.bfloat16)

    keys = project(key_near, key_whole, key_rest, "td,df->tf")
    queries = project(query_near, query_whole, query_rest, "td,df->ft")
    value_rest = along_x(others(value_whole), keys)
    values = project(value_near, value_whole, value_rest, "td,df->ft")
    out_near = along_x(out_pair)
    attended = [attend(queries, keys, values, peer_ids[0], bias, 1, width)]
    out_rest = along_x(others(out_whole), attended[0])
    attended.insert(0, attend(queries, keys, values, segments[0], bias, 0, width))
    attended = jnp.concatenate(attended, axis=1)

    side = place & 1
    stripes = own_width // (2 * w_out.shape[1])

    def sums(rows, mine):
        def block(step):
            first = (column ^ step) * stripes
            chosen = [
                lax.dynamic_slice_in_dim(rows, (mine ^ (first + j)) * half, half, 0)
                for j in range(stripes)
            ]
            chosen = chosen[0] if stripes == 1 else jnp.concatenate(chosen, axis=1)
            return jnp.einsum("ft,fc->tc", attended, chosen, preferred_element_type=jnp.float32)

        far = send(block(3), 1, "hidden")
        near = send(block(1), 1, "hidden")
        return block(0) + near, block(2) + far

    def send(value, step, axis="batch"):
        return swap(value.astype(jnp.bfloat16), step, axis).astype(jnp.float32)

    here, there = sums(out_whole, parity)
    first = here + send(there, 2, "hidden")
    first = first[:length] + send(first[length:], 2)
    here, there = sums(jnp.concatenate([out_near, out_rest], axis=0), place >> 1)
    there = there[:length] + send(there[length:], 2)
    second = here[:length] + send(here[length:], 2) + send(there, 2, "hidden")

    parts = [v.reshape(length, stripes, w_out.shape[1]) for v in (first, second)]
    combined = jnp.where(side == 0, jnp.stack(parts, 2), jnp.stack(parts[::-1], 2))
    return (tokens.astype(jnp.float32) + combined.reshape(length, own_width)).astype(jnp.bfloat16)


def solution(mesh):
    placed = (
        P("batch", "hidden"),
        P("batch", None),
        P(None, "hidden"),
        P(),
        P("batch", "hidden"),
        P("batch", "hidden"),
        P("batch", "hidden"),
        P("hidden", "batch"),
    )
    return jax.shard_map(
        functools.partial(per_device, mesh.shape["batch"], mesh.shape["hidden"]),
        mesh=mesh,
        in_specs=placed,
        out_specs=P("batch", "hidden"),
        check_vma=False,
    )
```

```python
import functools

import jax
import jax.numpy as jnp
from jax import lax
from jax.experimental import pallas as pl
from jax.experimental.pallas import tpu as pltpu
from jax.sharding import PartitionSpec as P

PASSAGE = 256
BLOCK = 128

norm_epsilon = 1e-06
bucket_edges = (12, 16, 23, 32, 46, 64, 91)
masked_score = -1e30


def bucket_of(offsets):
    distance = jnp.abs(offsets)
    reached = sum(((distance >= threshold).astype(jnp.int32) for threshold in bucket_edges))
    within = jnp.where(distance < 8, distance, 8 + reached)
    return within + jnp.where(offsets > 0, 16, 0)


def bias_tiles(table):
    rows = 2 * PASSAGE + BLOCK
    offsets = (
        jnp.arange(rows, dtype=jnp.int32)[:, None]
        - PASSAGE
        - jnp.arange(BLOCK, dtype=jnp.int32)[None, :]
    )
    buckets = bucket_of(offsets)[None]
    tiles = jnp.zeros((table.shape[1], rows, BLOCK), jnp.float32)
    for level in range(table.shape[0]):
        tiles = jnp.where(buckets == level, table[level][:, None, None], tiles)
    return tiles


def attention_kernel(width, q_ids, k_ids, bias, queries, keys, values, out):
    length = keys.shape[0]
    blocks = length // BLOCK
    reach = PASSAGE // BLOCK
    heads = keys.shape[1] // width
    for i in range(blocks):
        low, high = max(0, i - reach) * BLOCK, min(blocks, i + reach + 1) * BLOCK
        columns = slice(i * BLOCK, (i + 1) * BLOCK)
        first = low - i * BLOCK + PASSAGE
        same = k_ids[low:high, :] == q_ids[:, columns]
        for h in range(heads):
            rows = slice(h * width, (h + 1) * width)
            own = queries[rows, columns]
            blank = jnp.zeros_like(own)
            spread = jnp.concatenate([own if g == h else blank for g in range(heads)], axis=0)
            scores = jnp.dot(keys[low:high, :], spread, preferred_element_type=jnp.float32)
            scores = jnp.where(same, scores + bias[h, first : first + high - low, :], masked_score)
            raised = jnp.exp(scores - jnp.max(scores, axis=0, keepdims=True)).astype(jnp.bfloat16)
            extended = jnp.concatenate(
                [values[rows, low:high], jnp.ones((16, high - low), jnp.bfloat16)], axis=0
            )
            total = jnp.dot(extended, raised, preferred_element_type=jnp.float32)
            out[rows, columns] = (total[:width] / total[width : width + 1]).astype(jnp.bfloat16)


def attend(queries, keys, values, ids, bias, group, width):
    length = ids.shape[0]
    features = keys.shape[1]
    pair = 128 // width
    wide_ids = jnp.broadcast_to(ids[:, None], (length, BLOCK))
    return pl.pallas_call(
        functools.partial(attention_kernel, width),
        grid=(features // 128,),
        in_specs=[
            pl.BlockSpec((1, length), lambda p: (0, 0)),
            pl.BlockSpec((length, BLOCK), lambda p: (0, 0)),
            pl.BlockSpec((pair,) + bias.shape[1:], lambda p: (p, 0, 0)),
            pl.BlockSpec((128, length), lambda p: (p, group)),
            pl.BlockSpec((length, 128), lambda p: (group, p)),
            pl.BlockSpec((128, length), lambda p: (p, group)),
        ],
        out_specs=pl.BlockSpec((128, length), lambda p: (p, 0)),
        out_shape=jax.ShapeDtypeStruct((features, length), jnp.bfloat16),
        compiler_params=pltpu.CompilerParams(vmem_limit_bytes=24 * 1024 * 1024),
        cost_estimate=pl.CostEstimate(
            flops=8 * features * length * length,
            bytes_accessed=16 * features * length,
            transcendentals=features // width * length * length,
        ),
    )(ids[None, :], wide_ids, bias, queries, keys, values)


def after(value, earlier):
    return lax.optimization_barrier((value, earlier))[0]


def per_device(n_batch, n_hidden, tokens, segments, rel_bias, ln_gain, w_query, w_key, w_value, w_out):
    place = lax.axis_index("batch")
    column = lax.axis_index("hidden")
    parity = place & 1
    length, own_width = tokens.shape
    heads = rel_bias.shape[1] // 2
    half = w_query.shape[1] // 2
    width = half // heads

    def swap(value, step, axis="batch"):
        count = n_batch if axis == "batch" else n_hidden
        return lax.ppermute(value, axis, [(i, i ^ step) for i in range(count)])

    def swapped(weight, axis, *earlier):
        size = weight.shape[axis] // 2
        kept, given = [
            lax.dynamic_slice_in_dim(weight, side * size, size, axis)
            for side in (parity, 1 - parity)
        ]
        if earlier:
            given = after(given, earlier)
        taken = swap(given, 1)
        return jnp.where(parity == 0, kept, taken), jnp.where(parity == 0, taken, kept)

    def over_pairs(piece):
        groups = [[r + 2 * i for i in range(n_batch // 2)] for r in range(2)]
        return lax.all_gather(piece, "batch", axis=0, tiled=True, axis_index_groups=groups)

    key_pair = jnp.concatenate(swapped(w_key, 1), axis=0)

    peer_tokens = swap(after(tokens, key_pair), 1)
    peer_ids = swap(segments, 1)
    across = jnp.concatenate([swap(tokens, 2, "hidden"), swap(peer_tokens, 2, "hidden")], axis=0)
    held = jnp.concatenate([jnp.concatenate([tokens, peer_tokens], axis=0), across], axis=1)
    other = swap(held, 1, "hidden")

    query_pair = jnp.concatenate(swapped(w_query, 1, peer_tokens), axis=0)
    value_pair = jnp.concatenate(swapped(w_value, 1, query_pair), axis=0)
    out_pair = swapped(w_out, 0, value_pair)

    table = lax.dynamic_slice_in_dim(rel_bias, parity * heads, heads, 1)
    bias = bias_tiles(table)

    def squares(value):
        value = value.astype(jnp.float32)
        return jnp.sum(value * value, axis=1, keepdims=True)

    scale = lax.rsqrt((squares(held) + squares(other)) / (2 * held.shape[1]) + norm_epsilon)

    def normed_part(block):
        step = block ^ column
        where = (step >> 1) * own_width
        chosen = jnp.where(
            (step & 1) == 0,
            lax.dynamic_slice_in_dim(held, where, own_width, 1),
            lax.dynamic_slice_in_dim(other, where, own_width, 1),
        )
        gain = ln_gain[block * own_width : (block + 1) * own_width]
        return (chosen.astype(jnp.float32) * scale * gain).astype(jnp.bfloat16)

    normed = jnp.concatenate([normed_part(block) for block in range(n_hidden)], axis=1)

    def project(pair, form):
        total = jnp.einsum(form, normed, over_pairs(pair), preferred_element_type=jnp.float32)
        return total.astype(jnp.bfloat16)

    keys = project(key_pair, "td,df->tf")
    queries = project(query_pair, "td,df->ft")
    values = project(value_pair, "td,df->ft")
    w_out_even = over_pairs(after(out_pair[0], keys))
    w_out_odd = over_pairs(after(out_pair[1], queries))
    attended = jnp.concatenate(
        [
            attend(queries, keys, values, ids[0], bias, group, width)
            for group, ids in enumerate((segments, peer_ids))
        ],
        axis=1,
    )

    stripes = own_width // (2 * w_out.shape[1])

    def sums(rows):
        def block(step):
            first = (column ^ step) * stripes * half
            chosen = [
                lax.dynamic_slice_in_dim(rows, first + j * half, half, 0) for j in range(stripes)
            ]
            chosen = chosen[0] if stripes == 1 else jnp.concatenate(chosen, axis=1)
            return jnp.einsum("ft,fc->tc", attended, chosen, preferred_element_type=jnp.float32)

        far = send(block(3), 1, "hidden")
        near = send(block(1), 1, "hidden")
        return block(0) + near, block(2) + far

    def send(value, step, axis="batch"):
        return swap(value.astype(jnp.bfloat16), step, axis).astype(jnp.float32)

    here, there = sums(w_out_even)
    first = here + send(there, 2, "hidden")
    first = first[:length] + send(first[length:], 1)
    here, there = sums(w_out_odd)
    there = there[:length] + send(there[length:], 1)
    second = here[:length] + send(here[length:], 1) + send(there, 2, "hidden")

    parts = [v.reshape(length, stripes, w_out.shape[1]) for v in (first, second)]
    combined = jnp.stack(parts, 2)
    return (tokens.astype(jnp.float32) + combined.reshape(length, own_width)).astype(jnp.bfloat16)


def solution(mesh):
    placed = (
        P("batch", "hidden"),
        P("batch", None),
        P(None, "hidden"),
        P(),
        P("batch", "hidden"),
        P("batch", "hidden"),
        P("batch", "hidden"),
        P("hidden", "batch"),
    )
    return jax.shard_map(
        functools.partial(per_device, mesh.shape["batch"], mesh.shape["hidden"]),
        mesh=mesh,
        in_specs=placed,
        out_specs=P("batch", "hidden"),
        check_vma=False,
    )
```

```python
import functools

import jax
import jax.numpy as jnp
from jax import lax
from jax.experimental import pallas as pl
from jax.experimental.pallas import tpu as pltpu
from jax.sharding import PartitionSpec as P

PASSAGE = 256
BLOCK = 128

norm_epsilon = 1e-06
bucket_edges = (12, 16, 23, 32, 46, 64, 91)
masked_score = -1e30


def bucket_of(offsets):
    distance = jnp.abs(offsets)
    reached = sum(((distance >= threshold).astype(jnp.int32) for threshold in bucket_edges))
    within = jnp.where(distance < 8, distance, 8 + reached)
    return within + jnp.where(offsets > 0, 16, 0)


def bias_tiles(table):
    rows = 2 * PASSAGE + BLOCK
    offsets = (
        jnp.arange(rows, dtype=jnp.int32)[:, None]
        - PASSAGE
        - jnp.arange(BLOCK, dtype=jnp.int32)[None, :]
    )
    buckets = bucket_of(offsets)[None]
    tiles = jnp.zeros((table.shape[1], rows, BLOCK), jnp.float32)
    for level in range(table.shape[0]):
        tiles = jnp.where(buckets == level, table[level][:, None, None], tiles)
    return tiles


def attention_kernel(width, q_ids, k_ids, bias, queries, keys, values, out):
    length = keys.shape[0]
    blocks = length // BLOCK
    reach = PASSAGE // BLOCK
    heads = keys.shape[1] // width
    for i in range(blocks):
        low, high = max(0, i - reach) * BLOCK, min(blocks, i + reach + 1) * BLOCK
        columns = slice(i * BLOCK, (i + 1) * BLOCK)
        first = low - i * BLOCK + PASSAGE
        same = k_ids[low:high, :] == q_ids[:, columns]
        for h in range(heads):
            rows = slice(h * width, (h + 1) * width)
            own = queries[rows, columns]
            blank = jnp.zeros_like(own)
            spread = jnp.concatenate([own if g == h else blank for g in range(heads)], axis=0)
            scores = jnp.dot(keys[low:high, :], spread, preferred_element_type=jnp.float32)
            scores = jnp.where(same, scores + bias[h, first : first + high - low, :], masked_score)
            raised = jnp.exp(scores - jnp.max(scores, axis=0, keepdims=True)).astype(jnp.bfloat16)
            extended = jnp.concatenate(
                [values[rows, low:high], jnp.ones((16, high - low), jnp.bfloat16)], axis=0
            )
            total = jnp.dot(extended, raised, preferred_element_type=jnp.float32)
            out[rows, columns] = (total[:width] / total[width : width + 1]).astype(jnp.bfloat16)


def attend(queries, keys, values, ids, bias, group, width):
    length = ids.shape[0]
    features = keys.shape[1]
    pair = 128 // width
    wide_ids = jnp.broadcast_to(ids[:, None], (length, BLOCK))
    return pl.pallas_call(
        functools.partial(attention_kernel, width),
        grid=(features // 128,),
        in_specs=[
            pl.BlockSpec((1, length), lambda p: (0, 0)),
            pl.BlockSpec((length, BLOCK), lambda p: (0, 0)),
            pl.BlockSpec((pair,) + bias.shape[1:], lambda p: (p, 0, 0)),
            pl.BlockSpec((128, length), lambda p: (p, group)),
            pl.BlockSpec((length, 128), lambda p: (group, p)),
            pl.BlockSpec((128, length), lambda p: (p, group)),
        ],
        out_specs=pl.BlockSpec((128, length), lambda p: (p, 0)),
        out_shape=jax.ShapeDtypeStruct((features, length), jnp.bfloat16),
        compiler_params=pltpu.CompilerParams(vmem_limit_bytes=24 * 1024 * 1024),
        cost_estimate=pl.CostEstimate(
            flops=8 * features * length * length,
            bytes_accessed=16 * features * length,
            transcendentals=features // width * length * length,
        ),
    )(ids[None, :], wide_ids, bias, queries, keys, values)


def after(value, earlier):
    return lax.optimization_barrier((value, earlier))[0]


def per_device(n_batch, n_hidden, tokens, segments, rel_bias, ln_gain, w_query, w_key, w_value, w_out):
    place = lax.axis_index("batch")
    column = lax.axis_index("hidden")
    parity = place & 1
    length, own_width = tokens.shape
    heads = rel_bias.shape[1] // 2
    half = w_query.shape[1] // 2
    width = half // heads

    def swap(value, step, axis="batch"):
        count = n_batch if axis == "batch" else n_hidden
        return lax.ppermute(value, axis, [(i, i ^ step) for i in range(count)])

    pairs = n_batch // 2
    pair = place >> 1

    def swapped(weight, axis, *earlier):
        size = weight.shape[axis] // 2
        kept, given = [
            lax.dynamic_slice_in_dim(weight, side * size, size, axis)
            for side in (parity, 1 - parity)
        ]
        if earlier:
            given = after(given, earlier)
        taken = swap(given, 1)
        return jnp.where(parity == 0, jnp.concatenate([kept, taken]), jnp.concatenate([taken, kept]))

    def pass_on(value, way):
        return lax.ppermute(
            value, "batch", [(i, (i + 2 * way) % n_batch) for i in range(n_batch)]
        )

    def first_hops(block, *earlier):
        if earlier:
            block = after(block, earlier)
        return [pass_on(block, 1), pass_on(block, -1)]

    def round_ring(block, hops, *earlier):
        blocks = {0: block, pairs - 1: hops[0], 1: hops[1]}
        for step in range(2, pairs // 2):
            hops = [pass_on(hops[0], 1), pass_on(hops[1], -1)]
            blocks[pairs - step], blocks[step] = hops
        middle = block.shape[0] // 2
        ends = [hops[0][:middle], hops[1][middle:]]
        if earlier:
            ends = [after(end, wait) for end, wait in zip(ends, earlier)]
        blocks[pairs // 2] = jnp.concatenate([pass_on(ends[0], 1), pass_on(ends[1], -1)])
        return blocks

    key_block = swapped(w_key, 1)
    key_hops = first_hops(key_block)
    query_block = swapped(w_query, 1, key_block)
    query_hops = first_hops(query_block)

    peer_tokens = swap(after(tokens, key_block), 1)
    peer_ids = swap(segments, 1)
    across = swap(tokens, 2, "hidden")
    value_block = swapped(w_value, 1, peer_tokens)
    value_hops = first_hops(value_block, *key_hops, across)
    peer_across = swap(peer_tokens, 2, "hidden")
    out_block = swapped(w_out, 0, value_block)
    out_hops = first_hops(out_block, *query_hops, peer_across)

    def all_features(here, there):
        return [here, swap(here, 1, "hidden"), there, swap(there, 1, "hidden")]

    gathered = [all_features(tokens, across), all_features(peer_tokens, peer_across)]

    key_blocks = round_ring(key_block, key_hops)
    query_blocks = round_ring(query_block, query_hops)
    value_blocks = round_ring(value_block, value_hops, gathered[1][3], gathered[1][1])

    table = lax.dynamic_slice_in_dim(rel_bias, parity * heads, heads, 1)
    bias = bias_tiles(table)

    def normalised(parts):
        def squares(value):
            value = value.astype(jnp.float32)
            return jnp.sum(value * value, axis=1, keepdims=True)

        mean = sum(squares(part) for part in parts) / (own_width * len(parts))
        scale = lax.rsqrt(mean + norm_epsilon)
        gains = [
            lax.dynamic_slice_in_dim(ln_gain, (column ^ k) * own_width, own_width, 0)
            for k in range(len(parts))
        ]
        return jnp.concatenate(
            [
                (part.astype(jnp.float32) * scale * gain).astype(jnp.bfloat16)
                for part, gain in zip(parts, gains)
            ],
            axis=1,
        )

    normed = jnp.concatenate([normalised(parts) for parts in gathered], axis=0)
    depth = 2 * w_query.shape[0]

    def normed_part(offset):
        start = (pair + offset) % pairs * depth
        start = ((start // own_width) ^ column) * own_width + start % own_width
        return lax.dynamic_slice_in_dim(normed, start, depth, 1)

    arrival = [0] + [r for step in range(1, pairs // 2) for r in (pairs - step, step)] + [pairs // 2]
    size = max(1, pairs // 4)
    rounds = [arrival[i : i + size] for i in range(0, pairs, size)]

    def joined(values, axis):
        return values[0] if len(values) == 1 else jnp.concatenate(values, axis=axis)

    def project(blocks, form):
        total = None
        for offsets in rounds:
            part = joined([normed_part(r) for r in offsets], 1)
            rows = joined([blocks[r] for r in offsets], 0)
            term = jnp.einsum(form, part, rows, preferred_element_type=jnp.float32)
            total = term if total is None else total + term
        return total.astype(jnp.bfloat16)

    keys = project(key_blocks, "td,df->tf")
    queries = project(query_blocks, "td,df->ft")
    values = project(value_blocks, "td,df->ft")
    out_blocks = round_ring(out_block, out_hops, keys, queries)
    out_rows = jnp.concatenate([out_blocks[r] for r in range(pairs)], axis=0)
    attended = jnp.concatenate(
        [
            attend(queries, keys, values, ids[0], bias, group, width)
            for group, ids in enumerate((segments, peer_ids))
        ],
        axis=1,
    )

    stripes = own_width // (2 * w_out.shape[1])

    def sums(odd):
        def block(step):
            first = (column ^ step) * stripes
            chosen = [
                lax.dynamic_slice_in_dim(
                    out_rows, ((first + j - pair) % pairs * 2 + odd) * half, half, 0
                )
                for j in range(stripes)
            ]
            chosen = joined(chosen, 1)
            return jnp.einsum("ft,fc->tc", attended, chosen, preferred_element_type=jnp.float32)

        far = send(block(3), 1, "hidden")
        near = send(block(1), 1, "hidden")
        return block(0) + near, block(2) + far

    def send(value, step, axis="batch"):
        return swap(value.astype(jnp.bfloat16), step, axis).astype(jnp.float32)

    here, there = sums(0)
    first = here + send(there, 2, "hidden")
    first = first[:length] + send(first[length:], 1)
    here, there = sums(1)
    there = there[:length] + send(there[length:], 1)
    second = here[:length] + send(here[length:], 1) + send(there, 2, "hidden")

    parts = [v.reshape(length, stripes, w_out.shape[1]) for v in (first, second)]
    combined = jnp.stack(parts, 2)
    return (tokens.astype(jnp.float32) + combined.reshape(length, own_width)).astype(jnp.bfloat16)


def solution(mesh):
    placed = (
        P("batch", "hidden"),
        P("batch", None),
        P(None, "hidden"),
        P(),
        P("batch", "hidden"),
        P("batch", "hidden"),
        P("batch", "hidden"),
        P("hidden", "batch"),
    )
    return jax.shard_map(
        functools.partial(per_device, mesh.shape["batch"], mesh.shape["hidden"]),
        mesh=mesh,
        in_specs=placed,
        out_specs=P("batch", "hidden"),
        check_vma=False,
    )
```

```python
import functools

import jax
import jax.numpy as jnp
from jax import lax
from jax.experimental import pallas as pl
from jax.experimental.pallas import tpu as pltpu
from jax.sharding import PartitionSpec as P

PASSAGE = 256
BLOCK = 128

norm_epsilon = 1e-06
bucket_edges = (12, 16, 23, 32, 46, 64, 91)
masked_score = -1e30


def bucket_of(offsets):
    distance = jnp.abs(offsets)
    reached = sum(((distance >= threshold).astype(jnp.int32) for threshold in bucket_edges))
    within = jnp.where(distance < 8, distance, 8 + reached)
    return within + jnp.where(offsets > 0, 16, 0)


def bias_tiles(table):
    rows = 2 * PASSAGE + BLOCK
    offsets = (
        jnp.arange(rows, dtype=jnp.int32)[:, None]
        - PASSAGE
        - jnp.arange(BLOCK, dtype=jnp.int32)[None, :]
    )
    buckets = bucket_of(offsets)[None]
    tiles = jnp.zeros((table.shape[1], rows, BLOCK), jnp.float32)
    for level in range(table.shape[0]):
        tiles = jnp.where(buckets == level, table[level][:, None, None], tiles)
    return tiles


def attention_kernel(width, q_ids, k_ids, bias, queries, keys, values, out):
    length = keys.shape[0]
    blocks = length // BLOCK
    reach = PASSAGE // BLOCK
    heads = keys.shape[1] // width
    turned = jnp.transpose(values[...].astype(jnp.float32)).astype(jnp.bfloat16)
    head_of = lax.broadcasted_iota(jnp.int32, (BLOCK, keys.shape[1]), 1) // width
    for i in range(blocks):
        low, high = max(0, i - reach) * BLOCK, min(blocks, i + reach + 1) * BLOCK
        columns = slice(i * BLOCK, (i + 1) * BLOCK)
        first = low - i * BLOCK + PASSAGE
        same = k_ids[low:high, :] == q_ids[:, columns]
        own = queries[columns, :]
        results = []
        for h in range(heads):
            chosen = jnp.where(head_of == h, own, jnp.zeros_like(own))
            scores = lax.dot_general(
                keys[low:high, :],
                chosen,
                (((1,), (1,)), ((), ())),
                preferred_element_type=jnp.float32,
            )
            scores = jnp.where(same, scores + bias[h, first : first + high - low, :], masked_score)
            raised = jnp.exp(scores - jnp.max(scores, axis=0, keepdims=True)).astype(jnp.bfloat16)
            extended = jnp.concatenate(
                [
                    turned[h * width : (h + 1) * width, low:high],
                    jnp.ones((16, high - low), jnp.bfloat16),
                ],
                axis=0,
            )
            total = jnp.dot(extended, raised, preferred_element_type=jnp.float32)
            results.append(total[:width] / total[width : width + 1])
        out[columns, :] = jnp.transpose(jnp.concatenate(results, axis=0)).astype(jnp.bfloat16)


def attend(queries, keys, values, ids, bias, width):
    groups, length = ids.shape
    features = keys.shape[1]
    heads = 128 // width
    wide_ids = jnp.broadcast_to(ids.reshape(-1)[:, None], (groups * length, BLOCK))
    block = pl.BlockSpec((length, 128), lambda g, p: (g, p))
    return pl.pallas_call(
        functools.partial(attention_kernel, width),
        grid=(groups, features // 128),
        in_specs=[
            pl.BlockSpec((None, 1, length), lambda g, p: (g, 0, 0)),
            pl.BlockSpec((length, BLOCK), lambda g, p: (g, 0)),
            pl.BlockSpec((heads,) + bias.shape[1:], lambda g, p: (p, 0, 0)),
            block,
            block,
            block,
        ],
        out_specs=block,
        out_shape=jax.ShapeDtypeStruct(queries.shape, jnp.bfloat16),
        compiler_params=pltpu.CompilerParams(vmem_limit_bytes=24 * 1024 * 1024),
        cost_estimate=pl.CostEstimate(
            flops=8 * groups * features * length * length,
            bytes_accessed=16 * groups * features * length,
            transcendentals=groups * features // width * length * length,
        ),
    )(ids[:, None, :], wide_ids, bias, queries, keys, values)


def normalise_kernel(count, gains, *refs):
    out = refs[-1]
    for group in range(2):

        @pl.when(pl.program_id(0) == group)
        def _():
            parts = [
                ref[...].astype(jnp.float32) for ref in refs[group * count : (group + 1) * count]
            ]
            size = parts[0].shape[1]
            squares = sum(jnp.sum(part * part, axis=1, keepdims=True) for part in parts)
            scale = lax.rsqrt(squares / (size * count) + norm_epsilon)
            for k, part in enumerate(parts):
                out[:, k * size : (k + 1) * size] = (part * scale * gains[k : k + 1, :]).astype(
                    jnp.bfloat16
                )


def normalise(own, peer, gains):
    length, size = own[0].shape
    count = len(own)
    steps = length // BLOCK
    first = pl.BlockSpec((BLOCK, size), lambda g, i: (jnp.where(g == 0, i, steps - 1), 0))
    second = pl.BlockSpec((BLOCK, size), lambda g, i: (jnp.where(g == 0, 0, i), 0))
    return pl.pallas_call(
        functools.partial(normalise_kernel, count),
        grid=(2, steps),
        in_specs=[pl.BlockSpec(gains.shape, lambda g, i: (0, 0))]
        + [first] * count
        + [second] * count,
        out_specs=pl.BlockSpec((BLOCK, size * count), lambda g, i: (g * steps + i, 0)),
        out_shape=jax.ShapeDtypeStruct((2 * length, size * count), jnp.bfloat16),
        compiler_params=pltpu.CompilerParams(vmem_limit_bytes=24 * 1024 * 1024),
        cost_estimate=pl.CostEstimate(
            flops=16 * length * size * count,
            bytes_accessed=8 * length * size * count,
            transcendentals=2 * length,
        ),
    )(gains, *own, *peer)


def after(value, earlier):
    return lax.optimization_barrier((value, earlier))[0]


def per_device(n_batch, n_hidden, tokens, segments, rel_bias, ln_gain, w_query, w_key, w_value, w_out):
    place = lax.axis_index("batch")
    column = lax.axis_index("hidden")
    parity = place & 1
    length, own_width = tokens.shape
    heads = rel_bias.shape[1] // 2
    half = w_query.shape[1] // 2
    width = half // heads

    def swap(value, step, axis="batch"):
        count = n_batch if axis == "batch" else n_hidden
        return lax.ppermute(value, axis, [(i, i ^ step) for i in range(count)])

    pairs = n_batch // 2
    pair = place >> 1

    def swapped(weight, axis, *earlier):
        size = weight.shape[axis] // 2
        kept, given = [
            lax.dynamic_slice_in_dim(weight, side * size, size, axis)
            for side in (parity, 1 - parity)
        ]
        if earlier:
            given = after(given, earlier)
        taken = swap(given, 1)
        return jnp.where(parity == 0, jnp.concatenate([kept, taken]), jnp.concatenate([taken, kept]))

    def exchange(value, shift):
        def partner(i):
            other = ((i // 2 + shift) ^ 1) - shift
            return other % pairs * 2 + i % 2

        return lax.ppermute(value, "batch", [(i, partner(i)) for i in range(n_batch)])

    def meet(value, *earlier):
        if earlier:
            value = after(value, earlier)
        return [exchange(value, 0), exchange(value, 1)]

    sign = 1 - 2 * (pair & 1)
    steps = [0]
    for step in range(1, pairs // 2):
        steps += [step, -step] if step % 2 else [-step, step]
    steps.append(pairs // 2)

    def round_ring(block, received, *earlier):
        blocks, flows = [block, *received], list(received)
        for step in range(2, pairs // 2):
            flows = [exchange(flows[0], 1 - step % 2), exchange(flows[1], step % 2)]
            blocks += flows
        middle = block.shape[0] // 2
        ends = [flows[0][:middle], flows[1][middle:]]
        if earlier:
            ends = [after(end, wait) for end, wait in zip(ends, earlier)]
        blocks.append(jnp.concatenate([exchange(ends[0], 1), exchange(ends[1], 0)]))
        return blocks

    key_block = swapped(w_key, 1)
    key_hops = meet(key_block)
    query_block = swapped(w_query, 1, key_block)

    across = swap(tokens, 2, "hidden")
    peer_tokens = swap(after(tokens, key_block), 1)
    peer_ids = swap(segments, 1)
    query_hops = meet(query_block, across)
    peer_across = swap(after(peer_tokens, key_hops), 2, "hidden")
    value_block = swapped(w_value, 1, query_block)
    value_hops = meet(value_block, *key_hops)
    out_block = swapped(w_out, 0, value_block)
    out_hops = meet(out_block, *query_hops, peer_across)

    def all_features(here, there):
        return [here, swap(here, 1, "hidden"), there, swap(there, 1, "hidden")]

    gathered = [all_features(tokens, across), all_features(peer_tokens, peer_across)]

    key_blocks = round_ring(key_block, key_hops)
    query_blocks = round_ring(query_block, query_hops)
    value_blocks = round_ring(value_block, value_hops, gathered[1][3], gathered[1][1])

    table = lax.dynamic_slice_in_dim(rel_bias, parity * heads, heads, 1)
    bias = bias_tiles(table)

    gains = jnp.stack(
        [
            lax.dynamic_slice_in_dim(ln_gain, (column ^ k) * own_width, own_width, 0)
            for k in range(n_hidden)
        ]
    )
    normed = normalise(*gathered, gains)
    depth = 2 * w_query.shape[0]

    def normed_part(step):
        start = (pair + sign * step) % pairs * depth
        start = ((start // own_width) ^ column) * own_width + start % own_width
        return lax.dynamic_slice_in_dim(normed, start, depth, 1)

    size = max(1, pairs // 4)
    rounds = [slice(i, i + size) for i in range(0, pairs, size)]

    def joined(values, axis):
        return values[0] if len(values) == 1 else jnp.concatenate(values, axis=axis)

    def project(blocks):
        total = None
        for these in rounds:
            part = joined([normed_part(step) for step in steps[these]], 1)
            term = jnp.dot(part, joined(blocks[these], 0), preferred_element_type=jnp.float32)
            total = term if total is None else total + term
        return total.astype(jnp.bfloat16)

    keys = project(key_blocks)
    queries = project(query_blocks)
    values = project(value_blocks)
    out_blocks = round_ring(out_block, out_hops, keys, queries)
    place_of = {step % pairs: i for i, step in enumerate(steps)}
    out_rows = jnp.concatenate([out_blocks[place_of[e]] for e in range(pairs)], axis=0)
    ids = jnp.concatenate([segments, peer_ids], axis=0)
    attended = attend(queries, keys, values, ids, bias, width)

    stripes = own_width // (2 * w_out.shape[1])

    def sums(odd):
        def block(step):
            first = (column ^ step) * stripes
            chosen = [
                lax.dynamic_slice_in_dim(
                    out_rows, (sign * (first + j - pair) % pairs * 2 + odd) * half, half, 0
                )
                for j in range(stripes)
            ]
            chosen = joined(chosen, 1)
            return jnp.dot(attended, chosen, preferred_element_type=jnp.float32)

        far = send(block(3), 1, "hidden")
        near = send(block(1), 1, "hidden")
        return block(0) + near, block(2) + far

    def send(value, step, axis="batch"):
        return swap(value.astype(jnp.bfloat16), step, axis).astype(jnp.float32)

    here, there = sums(0)
    first = here + send(there, 2, "hidden")
    first = first[:length] + send(first[length:], 1)
    here, there = sums(1)
    there = there[:length] + send(there[length:], 1)
    second = here[:length] + send(here[length:], 1) + send(there, 2, "hidden")

    parts = [v.reshape(length, stripes, w_out.shape[1]) for v in (first, second)]
    combined = jnp.stack(parts, 2)
    return (tokens.astype(jnp.float32) + combined.reshape(length, own_width)).astype(jnp.bfloat16)


def solution(mesh):
    placed = (
        P("batch", "hidden"),
        P("batch", None),
        P(None, "hidden"),
        P(),
        P("batch", "hidden"),
        P("batch", "hidden"),
        P("batch", "hidden"),
        P("hidden", "batch"),
    )
    return jax.shard_map(
        functools.partial(per_device, mesh.shape["batch"], mesh.shape["hidden"]),
        mesh=mesh,
        in_specs=placed,
        out_specs=P("batch", "hidden"),
        check_vma=False,
    )
```

```python
import functools

import jax
import jax.numpy as jnp
from jax import lax
from jax.experimental import pallas as pl
from jax.experimental.pallas import tpu as pltpu
from jax.sharding import PartitionSpec as P

PASSAGE = 256
BLOCK = 128

norm_epsilon = 1e-06
bucket_edges = (12, 16, 23, 32, 46, 64, 91)
masked_score = -1e30


def bucket_of(offsets):
    distance = jnp.abs(offsets)
    reached = sum(((distance >= threshold).astype(jnp.int32) for threshold in bucket_edges))
    within = jnp.where(distance < 8, distance, 8 + reached)
    return within + jnp.where(offsets > 0, 16, 0)


def bias_tiles(table):
    rows = 2 * PASSAGE + BLOCK
    offsets = (
        jnp.arange(rows, dtype=jnp.int32)[:, None]
        - PASSAGE
        - jnp.arange(BLOCK, dtype=jnp.int32)[None, :]
    )
    buckets = bucket_of(offsets)[None]
    tiles = jnp.zeros((table.shape[1], rows, BLOCK), jnp.float32)
    for level in range(table.shape[0]):
        tiles = jnp.where(buckets == level, table[level][:, None, None], tiles)
    return tiles


def attention_kernel(width, q_ids, k_ids, bias, queries, keys, values, out):
    length = keys.shape[0]
    blocks = length // BLOCK
    reach = PASSAGE // BLOCK
    heads = keys.shape[1] // width
    turned = jnp.transpose(values[...].astype(jnp.float32)).astype(jnp.bfloat16)
    head_of = lax.broadcasted_iota(jnp.int32, (BLOCK, keys.shape[1]), 1) // width
    for i in range(blocks):
        low, high = max(0, i - reach) * BLOCK, min(blocks, i + reach + 1) * BLOCK
        columns = slice(i * BLOCK, (i + 1) * BLOCK)
        first = low - i * BLOCK + PASSAGE
        same = k_ids[low:high, :] == q_ids[:, columns]
        own = queries[columns, :]
        results = []
        for h in range(heads):
            chosen = jnp.where(head_of == h, own, jnp.zeros_like(own))
            scores = lax.dot_general(
                keys[low:high, :],
                chosen,
                (((1,), (1,)), ((), ())),
                preferred_element_type=jnp.float32,
            )
            scores = jnp.where(same, scores + bias[h, first : first + high - low, :], masked_score)
            raised = jnp.exp(scores - jnp.max(scores, axis=0, keepdims=True)).astype(jnp.bfloat16)
            extended = jnp.concatenate(
                [
                    turned[h * width : (h + 1) * width, low:high],
                    jnp.ones((16, high - low), jnp.bfloat16),
                ],
                axis=0,
            )
            total = jnp.dot(extended, raised, preferred_element_type=jnp.float32)
            results.append(total[:width] / total[width : width + 1])
        out[columns, :] = jnp.transpose(jnp.concatenate(results, axis=0)).astype(jnp.bfloat16)


def attend(queries, keys, values, ids, bias, width):
    groups, length = ids.shape
    features = keys.shape[1]
    heads = 128 // width
    wide_ids = jnp.broadcast_to(ids.reshape(-1)[:, None], (groups * length, BLOCK))
    block = pl.BlockSpec((length, 128), lambda g, p: (g, p))
    return pl.pallas_call(
        functools.partial(attention_kernel, width),
        grid=(groups, features // 128),
        in_specs=[
            pl.BlockSpec((None, 1, length), lambda g, p: (g, 0, 0)),
            pl.BlockSpec((length, BLOCK), lambda g, p: (g, 0)),
            pl.BlockSpec((heads,) + bias.shape[1:], lambda g, p: (p, 0, 0)),
            block,
            block,
            block,
        ],
        out_specs=block,
        out_shape=jax.ShapeDtypeStruct(queries.shape, jnp.bfloat16),
        compiler_params=pltpu.CompilerParams(vmem_limit_bytes=24 * 1024 * 1024),
        cost_estimate=pl.CostEstimate(
            flops=8 * groups * features * length * length,
            bytes_accessed=16 * groups * features * length,
            transcendentals=groups * features // width * length * length,
        ),
    )(ids[:, None, :], wide_ids, bias, queries, keys, values)


def normalise_kernel(sources, gain, own, peer, out):
    depth = out.shape[1] // sources.shape[0]
    for group, tokens in enumerate((own, peer)):

        @pl.when(pl.program_id(0) == group)
        def _():
            wide = tokens[...].astype(jnp.float32)
            scale = lax.rsqrt(jnp.mean(wide * wide, axis=1, keepdims=True) + norm_epsilon)
            for k in range(sources.shape[0]):
                start = pl.multiple_of(sources[k] * depth, 128)
                part = tokens[:, pl.ds(start, depth)].astype(jnp.float32)
                part = part * scale * gain[:, pl.ds(start, depth)]
                out[:, k * depth : (k + 1) * depth] = part.astype(jnp.bfloat16)


def normalise(own, peer, gain, sources):
    length, size = own.shape
    steps = length // BLOCK
    return pl.pallas_call(
        normalise_kernel,
        grid_spec=pltpu.PrefetchScalarGridSpec(
            num_scalar_prefetch=1,
            grid=(2, steps),
            in_specs=[
                pl.BlockSpec((1, size), lambda g, i, _: (0, 0)),
                pl.BlockSpec((BLOCK, size), lambda g, i, _: (jnp.where(g == 0, i, steps - 1), 0)),
                pl.BlockSpec((BLOCK, size), lambda g, i, _: (jnp.where(g == 0, 0, i), 0)),
            ],
            out_specs=pl.BlockSpec((BLOCK, size), lambda g, i, _: (g * steps + i, 0)),
        ),
        out_shape=jax.ShapeDtypeStruct((2 * length, size), jnp.bfloat16),
        compiler_params=pltpu.CompilerParams(vmem_limit_bytes=24 * 1024 * 1024),
        cost_estimate=pl.CostEstimate(
            flops=16 * length * size, bytes_accessed=8 * length * size, transcendentals=2 * length
        ),
    )(sources, gain[None, :], own, peer)


def after(value, earlier):
    return lax.optimization_barrier((value, earlier))[0]


def per_device(n_batch, n_hidden, tokens, segments, rel_bias, ln_gain, w_query, w_key, w_value, w_out):
    place = lax.axis_index("batch")
    column = lax.axis_index("hidden")
    parity = (place >> 1) & 1
    length, own_width = tokens.shape
    heads = rel_bias.shape[1] // 2
    half = w_query.shape[1] // 2
    width = half // heads

    def swap(value, step, axis="batch"):
        count = n_batch if axis == "batch" else n_hidden
        return lax.ppermute(value, axis, [(i, i ^ step) for i in range(count)])

    far = list(range(4, n_batch, 2))
    far_line, pair_line, near_line = [], [], []

    def paced(value, step, line, depth, *earlier):
        waits = tuple(line[-depth : len(line) - depth + 1]) + earlier
        if waits:
            value = after(value, waits)
        received = swap(value, step)
        line.append(received)
        return received

    def halves(weight, axis):
        size = weight.shape[axis] // 2
        return [
            lax.dynamic_slice_in_dim(weight, side * size, size, axis)
            for side in (parity, 1 - parity)
        ]

    def along_z(parts, waits):
        close = jnp.concatenate([parts[0], paced(parts[1], 2, pair_line, 1)], axis=0)
        distant = {
            step: paced(parts[(step >> 1) & 1], step, far_line, 2, *waits.get(step, ()))
            for step in reversed(far)
        }
        return close, jnp.concatenate([distant[step] for step in far], axis=0)

    def along_x(value, *earlier):
        return paced(value, 1, near_line, 2, *earlier)

    key_close, key_far = along_z(halves(w_key, 1), {})

    peer_tokens = paced(tokens, 2, pair_line, 1)
    peer_ids = swap(segments, 2)
    own_all, peer_all = [
        lax.all_gather(part, "hidden", axis=1, tiled=True) for part in (tokens, peer_tokens)
    ]

    query_close, query_far = along_z(halves(w_query, 1), {})
    key_near = along_x(key_close)
    query_near = along_x(query_close)
    key_rest = along_x(key_far)

    order = [0, 2] + far
    order += [step ^ 1 for step in order]
    normed = normalise(own_all, peer_all, ln_gain, jnp.stack([place ^ step for step in order]))

    value_close, value_far = along_z(halves(w_value, 1), {far[0]: (normed,)})
    value_near = along_x(value_close)
    query_rest = along_x(query_far)

    table = lax.dynamic_slice_in_dim(rel_bias, parity * heads, heads, 1)
    bias = bias_tiles(table)

    def joined(values, axis):
        return values[0] if len(values) == 1 else jnp.concatenate(values, axis=axis)

    def project(*blocks):
        total, first = None, 0
        for rows in blocks:
            part = normed[:, first : first + rows.shape[0]]
            first += rows.shape[0]
            term = jnp.dot(part, rows, preferred_element_type=jnp.float32)
            total = term if total is None else total + term
        return total.astype(jnp.bfloat16)

    keys = project(key_close, key_far, key_near, key_rest)
    queries = project(query_close, query_far, query_near, query_rest)
    out_close, out_far = along_z(halves(w_out, 0), {far[0]: (keys,)})
    out_near = along_x(out_close, keys)
    value_rest = along_x(value_far, queries)
    values = project(value_close, value_far, value_near, value_rest)
    out_rest = along_x(out_far, values)
    ids = jnp.concatenate([segments, peer_ids], axis=0)
    attended = attend(queries, keys, values, ids, bias, width)

    side = place & 1
    stripes = own_width // (2 * w_out.shape[1])

    def sums(rows):
        def block(step):
            first = (column ^ step) * stripes
            chosen = [
                lax.dynamic_slice_in_dim(rows, ((place >> 1) ^ (first + j)) * half, half, 0)
                for j in range(stripes)
            ]
            chosen = joined(chosen, 1)
            return jnp.dot(attended, chosen, preferred_element_type=jnp.float32)

        far = send(block(3), 1, "hidden")
        near = send(block(1), 1, "hidden")
        return block(0) + near, block(2) + far

    def send(value, step, axis="batch"):
        return swap(value.astype(jnp.bfloat16), step, axis).astype(jnp.float32)

    here, there = sums(jnp.concatenate([out_close, out_far], axis=0))
    first = here + send(there, 2, "hidden")
    first = first[:length] + send(first[length:], 2)
    here, there = sums(jnp.concatenate([out_near, out_rest], axis=0))
    there = there[:length] + send(there[length:], 2)
    second = here[:length] + send(here[length:], 2) + send(there, 2, "hidden")

    parts = [v.reshape(length, stripes, w_out.shape[1]) for v in (first, second)]
    combined = jnp.where(side == 0, jnp.stack(parts, 2), jnp.stack(parts[::-1], 2))
    return (tokens.astype(jnp.float32) + combined.reshape(length, own_width)).astype(jnp.bfloat16)


def solution(mesh):
    placed = (
        P("batch", "hidden"),
        P("batch", None),
        P(None, "hidden"),
        P(),
        P("batch", "hidden"),
        P("batch", "hidden"),
        P("batch", "hidden"),
        P("hidden", "batch"),
    )
    return jax.shard_map(
        functools.partial(per_device, mesh.shape["batch"], mesh.shape["hidden"]),
        mesh=mesh,
        in_specs=placed,
        out_specs=P("batch", "hidden"),
        check_vma=False,
    )
```

```python
import functools

import jax
import jax.numpy as jnp
from jax import lax
from jax.experimental import pallas as pl
from jax.experimental.pallas import tpu as pltpu
from jax.sharding import PartitionSpec as P

PASSAGE = 256
BLOCK = 128

norm_epsilon = 1e-06
bucket_edges = (12, 16, 23, 32, 46, 64, 91)
masked_score = -1e30


def bucket_of(offsets):
    distance = jnp.abs(offsets)
    reached = sum(((distance >= threshold).astype(jnp.int32) for threshold in bucket_edges))
    within = jnp.where(distance < 8, distance, 8 + reached)
    return within + jnp.where(offsets > 0, 16, 0)


def bias_tiles(table):
    rows = 2 * PASSAGE + BLOCK
    offsets = (
        jnp.arange(rows, dtype=jnp.int32)[:, None]
        - PASSAGE
        - jnp.arange(BLOCK, dtype=jnp.int32)[None, :]
    )
    buckets = bucket_of(offsets)[None]
    tiles = jnp.zeros((table.shape[1], rows, BLOCK), jnp.float32)
    for level in range(table.shape[0]):
        tiles = jnp.where(buckets == level, table[level][:, None, None], tiles)
    return tiles


def attention_kernel(width, q_ids, k_ids, bias, queries, keys, values, out):
    length = keys.shape[0]
    blocks = length // BLOCK
    reach = PASSAGE // BLOCK
    heads = keys.shape[1] // width
    turned = jnp.transpose(values[...].astype(jnp.float32)).astype(jnp.bfloat16)
    head_of = lax.broadcasted_iota(jnp.int32, (BLOCK, keys.shape[1]), 1) // width
    for i in range(blocks):
        low, high = max(0, i - reach) * BLOCK, min(blocks, i + reach + 1) * BLOCK
        columns = slice(i * BLOCK, (i + 1) * BLOCK)
        first = low - i * BLOCK + PASSAGE
        same = k_ids[low:high, :] == q_ids[:, columns]
        own = queries[columns, :]
        results = []
        for h in range(heads):
            chosen = jnp.where(head_of == h, own, jnp.zeros_like(own))
            scores = lax.dot_general(
                keys[low:high, :],
                chosen,
                (((1,), (1,)), ((), ())),
                preferred_element_type=jnp.float32,
            )
            scores = jnp.where(same, scores + bias[h, first : first + high - low, :], masked_score)
            raised = jnp.exp(scores - jnp.max(scores, axis=0, keepdims=True)).astype(jnp.bfloat16)
            extended = jnp.concatenate(
                [
                    turned[h * width : (h + 1) * width, low:high],
                    jnp.ones((16, high - low), jnp.bfloat16),
                ],
                axis=0,
            )
            total = jnp.dot(extended, raised, preferred_element_type=jnp.float32)
            results.append(total[:width] / total[width : width + 1])
        out[columns, :] = jnp.transpose(jnp.concatenate(results, axis=0)).astype(jnp.bfloat16)


def attend(queries, keys, values, ids, bias, width):
    groups, length = ids.shape
    features = keys.shape[1]
    heads = 128 // width
    wide_ids = jnp.broadcast_to(ids.reshape(-1)[:, None], (groups * length, BLOCK))
    block = pl.BlockSpec((length, 128), lambda g, p: (g, p))
    return pl.pallas_call(
        functools.partial(attention_kernel, width),
        grid=(groups, features // 128),
        in_specs=[
            pl.BlockSpec((None, 1, length), lambda g, p: (g, 0, 0)),
            pl.BlockSpec((length, BLOCK), lambda g, p: (g, 0)),
            pl.BlockSpec((heads,) + bias.shape[1:], lambda g, p: (p, 0, 0)),
            block,
            block,
            block,
        ],
        out_specs=block,
        out_shape=jax.ShapeDtypeStruct(queries.shape, jnp.bfloat16),
        compiler_params=pltpu.CompilerParams(vmem_limit_bytes=24 * 1024 * 1024),
        cost_estimate=pl.CostEstimate(
            flops=8 * groups * features * length * length,
            bytes_accessed=16 * groups * features * length,
            transcendentals=groups * features // width * length * length,
        ),
    )(ids[:, None, :], wide_ids, bias, queries, keys, values)


def normalise_kernel(sources, gain, own, peer, out):
    depth = out.shape[1] // sources.shape[0]
    for group, tokens in enumerate((own, peer)):

        @pl.when(pl.program_id(0) == group)
        def _():
            wide = tokens[...].astype(jnp.float32)
            scale = lax.rsqrt(jnp.mean(wide * wide, axis=1, keepdims=True) + norm_epsilon)
            for k in range(sources.shape[0]):
                start = pl.multiple_of(sources[k] * depth, 128)
                part = tokens[:, pl.ds(start, depth)].astype(jnp.float32)
                part = part * scale * gain[:, pl.ds(start, depth)]
                out[:, k * depth : (k + 1) * depth] = part.astype(jnp.bfloat16)


def normalise(own, peer, gain, sources):
    length, size = own.shape
    steps = length // BLOCK
    return pl.pallas_call(
        normalise_kernel,
        grid_spec=pltpu.PrefetchScalarGridSpec(
            num_scalar_prefetch=1,
            grid=(2, steps),
            in_specs=[
                pl.BlockSpec((1, size), lambda g, i, _: (0, 0)),
                pl.BlockSpec((BLOCK, size), lambda g, i, _: (jnp.where(g == 0, i, steps - 1), 0)),
                pl.BlockSpec((BLOCK, size), lambda g, i, _: (jnp.where(g == 0, 0, i), 0)),
            ],
            out_specs=pl.BlockSpec((BLOCK, size), lambda g, i, _: (g * steps + i, 0)),
        ),
        out_shape=jax.ShapeDtypeStruct((2 * length, size), jnp.bfloat16),
        compiler_params=pltpu.CompilerParams(vmem_limit_bytes=24 * 1024 * 1024),
        cost_estimate=pl.CostEstimate(
            flops=16 * length * size, bytes_accessed=8 * length * size, transcendentals=2 * length
        ),
    )(sources, gain[None, :], own, peer)


def after(value, earlier):
    return lax.optimization_barrier((value, earlier))[0]


def per_device(n_batch, n_hidden, tokens, segments, rel_bias, ln_gain, w_query, w_key, w_value, w_out):
    place = lax.axis_index("batch")
    column = lax.axis_index("hidden")
    parity = (place >> 1) & 1
    length, own_width = tokens.shape
    heads = rel_bias.shape[1] // 2
    half = w_query.shape[1] // 2
    width = half // heads

    def swap(value, step, axis="batch"):
        count = n_batch if axis == "batch" else n_hidden
        return lax.ppermute(value, axis, [(i, i ^ step) for i in range(count)])

    far = list(range(4, n_batch, 2))
    far_line, pair_line, near_line = [], [], []

    def paced(value, step, line, depth, *earlier):
        waits = tuple(line[-depth : len(line) - depth + 1]) + earlier
        if waits:
            value = after(value, waits)
        received = swap(value, step)
        line.append(received)
        return received

    def halves(weight, axis):
        size = weight.shape[axis] // 2
        return [
            lax.dynamic_slice_in_dim(weight, side * size, size, axis)
            for side in (parity, 1 - parity)
        ]

    def along_z(parts, waits={}):
        distant = {
            step: paced(parts[(step >> 1) & 1], step, far_line, 2, *waits.get(step, ()))
            for step in reversed(far)
        }
        close = jnp.concatenate([parts[0], paced(parts[1], 2, pair_line, 1)], axis=0)
        return close, jnp.concatenate([distant[step] for step in far], axis=0)

    def along_x(value, *earlier):
        return paced(value, 1, near_line, 2, *earlier)

    key_close, key_far = along_z(halves(w_key, 1))
    query_close, query_far = along_z(halves(w_query, 1))

    peer_tokens = paced(tokens, 2, pair_line, 1, far_line[0])
    peer_ids = swap(segments, 2)
    own_all, peer_all = [
        lax.all_gather(part, "hidden", axis=1, tiled=True) for part in (tokens, peer_tokens)
    ]

    key_near = along_x(key_close)
    query_near = along_x(query_close)
    key_rest = along_x(key_far)

    order = [0, 2] + far
    order += [step ^ 1 for step in order]
    normed = normalise(own_all, peer_all, ln_gain, jnp.stack([place ^ step for step in order]))

    value_close, value_far = along_z(
        halves(w_value, 1), {far[-1]: (key_near,), far[0]: (query_near,)}
    )
    value_near = along_x(value_close)
    query_rest = along_x(query_far, normed)

    table = lax.dynamic_slice_in_dim(rel_bias, parity * heads, heads, 1)
    bias = bias_tiles(table)

    def joined(values, axis):
        return values[0] if len(values) == 1 else jnp.concatenate(values, axis=axis)

    def project(*blocks):
        total, first = None, 0
        for rows in blocks:
            part = normed[:, first : first + rows.shape[0]]
            first += rows.shape[0]
            term = jnp.dot(part, rows, preferred_element_type=jnp.float32)
            total = term if total is None else total + term
        return total.astype(jnp.bfloat16)

    keys = project(key_close, key_far, key_near, key_rest)
    queries = project(query_close, query_far, query_near, query_rest)
    out_close, out_far = along_z(
        halves(w_out, 0), {far[-1]: (key_rest,), far[0]: (value_near, normed)}
    )
    out_near = along_x(out_close, keys)
    value_rest = along_x(value_far, queries)
    values = project(value_close, value_far, value_near, value_rest)
    out_rest = along_x(out_far, values)
    ids = jnp.concatenate([segments, peer_ids], axis=0)
    attended = attend(queries, keys, values, ids, bias, width)

    side = place & 1
    stripes = own_width // (2 * w_out.shape[1])

    def sums(rows):
        def block(step):
            first = (column ^ step) * stripes
            chosen = [
                lax.dynamic_slice_in_dim(rows, ((place >> 1) ^ (first + j)) * half, half, 0)
                for j in range(stripes)
            ]
            chosen = joined(chosen, 1)
            return jnp.dot(attended, chosen, preferred_element_type=jnp.float32)

        far = send(block(3), 1, "hidden")
        near = send(block(1), 1, "hidden")
        return block(0) + near, block(2) + far

    def send(value, step, axis="batch"):
        return swap(value.astype(jnp.bfloat16), step, axis).astype(jnp.float32)

    here, there = sums(jnp.concatenate([out_close, out_far], axis=0))
    first = here + send(there, 2, "hidden")
    here, there = sums(jnp.concatenate([out_near, out_rest], axis=0))
    there_peer = send(there[length:], 2)
    here_peer = send(here[length:], 2)
    second = here[:length] + here_peer + send(there[:length] + there_peer, 2, "hidden")
    first_peer = after(first[length:].astype(jnp.bfloat16), (there_peer, here_peer))
    first = first[:length] + send(first_peer, 2)

    parts = [v.reshape(length, stripes, w_out.shape[1]) for v in (first, second)]
    combined = jnp.where(side == 0, jnp.stack(parts, 2), jnp.stack(parts[::-1], 2))
    return (tokens.astype(jnp.float32) + combined.reshape(length, own_width)).astype(jnp.bfloat16)


def solution(mesh):
    placed = (
        P("batch", "hidden"),
        P("batch", None),
        P(None, "hidden"),
        P(),
        P("batch", "hidden"),
        P("batch", "hidden"),
        P("batch", "hidden"),
        P("hidden", "batch"),
    )
    return jax.shard_map(
        functools.partial(per_device, mesh.shape["batch"], mesh.shape["hidden"]),
        mesh=mesh,
        in_specs=placed,
        out_specs=P("batch", "hidden"),
        check_vma=False,
    )
```

```python
import functools

import jax
import jax.numpy as jnp
from jax import lax
from jax.experimental import pallas as pl
from jax.experimental.pallas import tpu as pltpu
from jax.sharding import PartitionSpec as P

PASSAGE = 256
BLOCK = 128

norm_epsilon = 1e-06
bucket_edges = (12, 16, 23, 32, 46, 64, 91)
masked_score = -1e30


def bucket_of(offsets):
    distance = jnp.abs(offsets)
    reached = sum(((distance >= threshold).astype(jnp.int32) for threshold in bucket_edges))
    within = jnp.where(distance < 8, distance, 8 + reached)
    return within + jnp.where(offsets > 0, 16, 0)


def bias_tiles(table):
    rows = 2 * PASSAGE + BLOCK
    offsets = (
        jnp.arange(rows, dtype=jnp.int32)[:, None]
        - PASSAGE
        - jnp.arange(BLOCK, dtype=jnp.int32)[None, :]
    )
    buckets = bucket_of(offsets)[None]
    tiles = jnp.zeros((table.shape[1], rows, BLOCK), jnp.float32)
    for level in range(table.shape[0]):
        tiles = jnp.where(buckets == level, table[level][:, None, None], tiles)
    return tiles


def attention_kernel(width, q_ids, k_ids, bias, queries, keys, values, out):
    length = keys.shape[0]
    blocks = length // BLOCK
    reach = PASSAGE // BLOCK
    heads = keys.shape[1] // width
    turned = jnp.transpose(values[...].astype(jnp.float32)).astype(jnp.bfloat16)
    head_of = lax.broadcasted_iota(jnp.int32, (BLOCK, keys.shape[1]), 1) // width
    for i in range(blocks):
        low, high = max(0, i - reach) * BLOCK, min(blocks, i + reach + 1) * BLOCK
        columns = slice(i * BLOCK, (i + 1) * BLOCK)
        first = low - i * BLOCK + PASSAGE
        same = k_ids[low:high, :] == q_ids[:, columns]
        own = queries[columns, :]
        results = []
        for h in range(heads):
            chosen = jnp.where(head_of == h, own, jnp.zeros_like(own))
            scores = lax.dot_general(
                keys[low:high, :],
                chosen,
                (((1,), (1,)), ((), ())),
                preferred_element_type=jnp.float32,
            )
            scores = jnp.where(same, scores + bias[h, first : first + high - low, :], masked_score)
            raised = jnp.exp(scores - jnp.max(scores, axis=0, keepdims=True)).astype(jnp.bfloat16)
            extended = jnp.concatenate(
                [
                    turned[h * width : (h + 1) * width, low:high],
                    jnp.ones((16, high - low), jnp.bfloat16),
                ],
                axis=0,
            )
            total = jnp.dot(extended, raised, preferred_element_type=jnp.float32)
            results.append(total[:width] / total[width : width + 1])
        out[columns, :] = jnp.transpose(jnp.concatenate(results, axis=0)).astype(jnp.bfloat16)


def attend(queries, keys, values, ids, bias, width):
    groups, length = ids.shape
    features = keys.shape[1]
    heads = 128 // width
    wide_ids = jnp.broadcast_to(ids.reshape(-1)[:, None], (groups * length, BLOCK))
    block = pl.BlockSpec((length, 128), lambda g, p: (g, p))
    return pl.pallas_call(
        functools.partial(attention_kernel, width),
        grid=(groups, features // 128),
        in_specs=[
            pl.BlockSpec((None, 1, length), lambda g, p: (g, 0, 0)),
            pl.BlockSpec((length, BLOCK), lambda g, p: (g, 0)),
            pl.BlockSpec((heads,) + bias.shape[1:], lambda g, p: (p, 0, 0)),
            block,
            block,
            block,
        ],
        out_specs=block,
        out_shape=jax.ShapeDtypeStruct(queries.shape, jnp.bfloat16),
        compiler_params=pltpu.CompilerParams(vmem_limit_bytes=24 * 1024 * 1024),
        cost_estimate=pl.CostEstimate(
            flops=8 * groups * features * length * length,
            bytes_accessed=16 * groups * features * length,
            transcendentals=groups * features // width * length * length,
        ),
    )(ids[:, None, :], wide_ids, bias, queries, keys, values)


def normalise_kernel(sources, gain, own, peer, out):
    depth = out.shape[1] // sources.shape[0]
    for group, tokens in enumerate((own, peer)):

        @pl.when(pl.program_id(0) == group)
        def _():
            wide = tokens[...].astype(jnp.float32)
            scale = lax.rsqrt(jnp.mean(wide * wide, axis=1, keepdims=True) + norm_epsilon)
            for k in range(sources.shape[0]):
                start = pl.multiple_of(sources[k] * depth, 128)
                part = tokens[:, pl.ds(start, depth)].astype(jnp.float32)
                part = part * scale * gain[:, pl.ds(start, depth)]
                out[:, k * depth : (k + 1) * depth] = part.astype(jnp.bfloat16)


def normalise(own, peer, gain, sources):
    length, size = own.shape
    steps = length // BLOCK
    return pl.pallas_call(
        normalise_kernel,
        grid_spec=pltpu.PrefetchScalarGridSpec(
            num_scalar_prefetch=1,
            grid=(2, steps),
            in_specs=[
                pl.BlockSpec((1, size), lambda g, i, _: (0, 0)),
                pl.BlockSpec((BLOCK, size), lambda g, i, _: (jnp.where(g == 0, i, steps - 1), 0)),
                pl.BlockSpec((BLOCK, size), lambda g, i, _: (jnp.where(g == 0, 0, i), 0)),
            ],
            out_specs=pl.BlockSpec((BLOCK, size), lambda g, i, _: (g * steps + i, 0)),
        ),
        out_shape=jax.ShapeDtypeStruct((2 * length, size), jnp.bfloat16),
        compiler_params=pltpu.CompilerParams(vmem_limit_bytes=24 * 1024 * 1024),
        cost_estimate=pl.CostEstimate(
            flops=16 * length * size, bytes_accessed=8 * length * size, transcendentals=2 * length
        ),
    )(sources, gain[None, :], own, peer)


def after(value, earlier):
    return lax.optimization_barrier((value, earlier))[0]


def per_device(n_batch, n_hidden, tokens, segments, rel_bias, ln_gain, w_query, w_key, w_value, w_out):
    place = lax.axis_index("batch")
    column = lax.axis_index("hidden")
    parity = (place >> 1) & 1
    length, own_width = tokens.shape
    heads = rel_bias.shape[1] // 2
    half = w_query.shape[1] // 2
    width = half // heads

    def swap(value, step, axis="batch"):
        count = n_batch if axis == "batch" else n_hidden
        return lax.ppermute(value, axis, [(i, i ^ step) for i in range(count)])

    far = list(range(4, n_batch, 2))
    far_line, pair_line, near_line = [], [], []

    def paced(value, step, line, depth, *earlier):
        waits = tuple(line[-depth : len(line) - depth + 1]) + earlier
        if waits:
            value = after(value, waits)
        received = swap(value, step)
        line.append(received)
        return received

    def halves(weight, axis):
        size = weight.shape[axis] // 2
        return [
            lax.dynamic_slice_in_dim(weight, side * size, size, axis)
            for side in (parity, 1 - parity)
        ]

    def close_by(parts):
        return jnp.concatenate([parts[0], paced(parts[1], 2, pair_line, 1)], axis=0)

    def far_off(parts):
        distant = {
            step: paced(parts[(step >> 1) & 1], step, far_line, 2) for step in reversed(far)
        }
        return jnp.concatenate([distant[step] for step in far], axis=0)

    def gathered(close):
        planes = n_batch // 4
        size = close.shape[0]
        groups = [[r + 4 * i for i in range(planes)] for r in range(4)]
        whole = lax.all_gather(close, "batch", axis=0, tiled=True, axis_index_groups=groups)
        rest = [
            lax.dynamic_slice_in_dim(whole, ((place >> 2) ^ k) * size, size, 0)
            for k in range(1, planes)
        ]
        return rest[0] if len(rest) == 1 else jnp.concatenate(rest, axis=0)

    def along_x(value, *earlier):
        return paced(value, 1, near_line, 2, *earlier)

    peer_tokens = paced(tokens, 2, pair_line, 1)
    peer_ids = swap(segments, 2)
    own_all, peer_all = [
        lax.all_gather(part, "hidden", axis=1, tiled=True) for part in (tokens, peer_tokens)
    ]

    key_parts, query_parts = halves(w_key, 1), halves(w_query, 1)
    key_close = close_by(key_parts)
    key_far = far_off(key_parts)
    query_close = close_by(query_parts)
    query_far = far_off(query_parts)
    value_close = close_by(halves(w_value, 1))
    out_close = close_by(halves(w_out, 0))

    key_near = along_x(key_close)
    query_near = along_x(query_close)
    value_far = gathered(after(value_close, (own_all, far_line[0])))
    key_rest = along_x(key_far)
    value_near = along_x(value_close)
    query_rest = along_x(query_far)

    order = [0, 2] + far
    order += [step ^ 1 for step in order]
    normed = normalise(own_all, peer_all, ln_gain, jnp.stack([place ^ step for step in order]))

    table = lax.dynamic_slice_in_dim(rel_bias, parity * heads, heads, 1)
    bias = bias_tiles(table)

    def joined(values, axis):
        return values[0] if len(values) == 1 else jnp.concatenate(values, axis=axis)

    def project(*blocks):
        total, first = None, 0
        for rows in blocks:
            part = normed[:, first : first + rows.shape[0]]
            first += rows.shape[0]
            term = jnp.dot(part, rows, preferred_element_type=jnp.float32)
            total = term if total is None else total + term
        return total.astype(jnp.bfloat16)

    keys = project(key_close, key_far, key_near, key_rest)
    queries = project(query_close, query_far, query_near, query_rest)
    out_far = gathered(after(out_close, keys))
    out_near = along_x(out_close, normed)
    value_rest = along_x(value_far, normed)
    values = project(value_close, value_far, value_near, value_rest)
    out_rest = along_x(out_far, values)
    ids = jnp.concatenate([segments, peer_ids], axis=0)
    attended = attend(queries, keys, values, ids, bias, width)

    side = place & 1
    stripes = own_width // (2 * w_out.shape[1])

    def sums(rows):
        def block(step):
            first = (column ^ step) * stripes
            chosen = [
                lax.dynamic_slice_in_dim(rows, ((place >> 1) ^ (first + j)) * half, half, 0)
                for j in range(stripes)
            ]
            chosen = joined(chosen, 1)
            return jnp.dot(attended, chosen, preferred_element_type=jnp.float32)

        far = send(block(3), 1, "hidden")
        near = send(block(1), 1, "hidden")
        return block(0) + near, block(2) + far

    def send(value, step, axis="batch"):
        return swap(value.astype(jnp.bfloat16), step, axis).astype(jnp.float32)

    here, there = sums(jnp.concatenate([out_close, out_far], axis=0))
    first = here + send(there, 2, "hidden")
    here, there = sums(jnp.concatenate([out_near, out_rest], axis=0))
    there_peer = send(there[length:], 2)
    here_peer = send(here[length:], 2)
    second = here[:length] + here_peer + send(there[:length] + there_peer, 2, "hidden")
    first_peer = after(first[length:].astype(jnp.bfloat16), (there_peer, here_peer))
    first = first[:length] + send(first_peer, 2)

    parts = [v.reshape(length, stripes, w_out.shape[1]) for v in (first, second)]
    combined = jnp.where(side == 0, jnp.stack(parts, 2), jnp.stack(parts[::-1], 2))
    return (tokens.astype(jnp.float32) + combined.reshape(length, own_width)).astype(jnp.bfloat16)


def solution(mesh):
    placed = (
        P("batch", "hidden"),
        P("batch", None),
        P(None, "hidden"),
        P(),
        P("batch", "hidden"),
        P("batch", "hidden"),
        P("batch", "hidden"),
        P("hidden", "batch"),
    )
    return jax.shard_map(
        functools.partial(per_device, mesh.shape["batch"], mesh.shape["hidden"]),
        mesh=mesh,
        in_specs=placed,
        out_specs=P("batch", "hidden"),
        check_vma=False,
    )
```

```python
import functools

import jax
import jax.numpy as jnp
from jax import lax
from jax.experimental import pallas as pl
from jax.experimental.pallas import tpu as pltpu
from jax.sharding import PartitionSpec as P

PASSAGE = 256
BLOCK = 128

norm_epsilon = 1e-06
bucket_edges = (12, 16, 23, 32, 46, 64, 91)
masked_score = -1e30


def bucket_of(offsets):
    distance = jnp.abs(offsets)
    reached = sum(((distance >= threshold).astype(jnp.int32) for threshold in bucket_edges))
    within = jnp.where(distance < 8, distance, 8 + reached)
    return within + jnp.where(offsets > 0, 16, 0)


def bias_tiles(table):
    rows = 2 * PASSAGE + BLOCK
    offsets = (
        jnp.arange(rows, dtype=jnp.int32)[:, None]
        - PASSAGE
        - jnp.arange(BLOCK, dtype=jnp.int32)[None, :]
    )
    buckets = bucket_of(offsets)[None]
    tiles = jnp.zeros((table.shape[1], rows, BLOCK), jnp.float32)
    for level in range(table.shape[0]):
        tiles = jnp.where(buckets == level, table[level][:, None, None], tiles)
    return tiles


def attention_kernel(width, q_ids, k_ids, bias, queries, keys, values, out):
    length = keys.shape[0]
    blocks = length // BLOCK
    reach = PASSAGE // BLOCK
    heads = keys.shape[1] // width
    turned = jnp.transpose(values[...].astype(jnp.float32)).astype(jnp.bfloat16)
    head_of = lax.broadcasted_iota(jnp.int32, (BLOCK, keys.shape[1]), 1) // width
    for i in range(blocks):
        low, high = max(0, i - reach) * BLOCK, min(blocks, i + reach + 1) * BLOCK
        columns = slice(i * BLOCK, (i + 1) * BLOCK)
        first = low - i * BLOCK + PASSAGE
        same = k_ids[low:high, :] == q_ids[:, columns]
        own = queries[columns, :]
        results = []
        for h in range(heads):
            chosen = jnp.where(head_of == h, own, jnp.zeros_like(own))
            scores = lax.dot_general(
                keys[low:high, :],
                chosen,
                (((1,), (1,)), ((), ())),
                preferred_element_type=jnp.float32,
            )
            scores = jnp.where(same, scores + bias[h, first : first + high - low, :], masked_score)
            raised = jnp.exp(scores - jnp.max(scores, axis=0, keepdims=True)).astype(jnp.bfloat16)
            extended = jnp.concatenate(
                [
                    turned[h * width : (h + 1) * width, low:high],
                    jnp.ones((16, high - low), jnp.bfloat16),
                ],
                axis=0,
            )
            total = jnp.dot(extended, raised, preferred_element_type=jnp.float32)
            results.append(total[:width] / total[width : width + 1])
        out[columns, :] = jnp.transpose(jnp.concatenate(results, axis=0)).astype(jnp.bfloat16)


def attend(queries, keys, values, ids, bias, width):
    groups, length = ids.shape
    features = keys.shape[1]
    heads = 128 // width
    wide_ids = jnp.broadcast_to(ids.reshape(-1)[:, None], (groups * length, BLOCK))
    block = pl.BlockSpec((length, 128), lambda g, p: (g, p))
    return pl.pallas_call(
        functools.partial(attention_kernel, width),
        grid=(groups, features // 128),
        in_specs=[
            pl.BlockSpec((None, 1, length), lambda g, p: (g, 0, 0)),
            pl.BlockSpec((length, BLOCK), lambda g, p: (g, 0)),
            pl.BlockSpec((heads,) + bias.shape[1:], lambda g, p: (p, 0, 0)),
            block,
            block,
            block,
        ],
        out_specs=block,
        out_shape=jax.ShapeDtypeStruct(queries.shape, jnp.bfloat16),
        compiler_params=pltpu.CompilerParams(vmem_limit_bytes=24 * 1024 * 1024),
        cost_estimate=pl.CostEstimate(
            flops=8 * groups * features * length * length,
            bytes_accessed=16 * groups * features * length,
            transcendentals=groups * features // width * length * length,
        ),
    )(ids[:, None, :], wide_ids, bias, queries, keys, values)


def normalise_kernel(sources, gain, own, peer, out):
    depth = out.shape[1] // sources.shape[0]
    for group, tokens in enumerate((own, peer)):

        @pl.when(pl.program_id(0) == group)
        def _():
            wide = tokens[...].astype(jnp.float32)
            scale = lax.rsqrt(jnp.mean(wide * wide, axis=1, keepdims=True) + norm_epsilon)
            for k in range(sources.shape[0]):
                start = pl.multiple_of(sources[k] * depth, 128)
                part = tokens[:, pl.ds(start, depth)].astype(jnp.float32)
                part = part * scale * gain[:, pl.ds(start, depth)]
                out[:, k * depth : (k + 1) * depth] = part.astype(jnp.bfloat16)


def normalise(own, peer, gain, sources):
    length, size = own.shape
    steps = length // BLOCK
    return pl.pallas_call(
        normalise_kernel,
        grid_spec=pltpu.PrefetchScalarGridSpec(
            num_scalar_prefetch=1,
            grid=(2, steps),
            in_specs=[
                pl.BlockSpec((1, size), lambda g, i, _: (0, 0)),
                pl.BlockSpec((BLOCK, size), lambda g, i, _: (jnp.where(g == 0, i, steps - 1), 0)),
                pl.BlockSpec((BLOCK, size), lambda g, i, _: (jnp.where(g == 0, 0, i), 0)),
            ],
            out_specs=pl.BlockSpec((BLOCK, size), lambda g, i, _: (g * steps + i, 0)),
        ),
        out_shape=jax.ShapeDtypeStruct((2 * length, size), jnp.bfloat16),
        compiler_params=pltpu.CompilerParams(vmem_limit_bytes=24 * 1024 * 1024),
        cost_estimate=pl.CostEstimate(
            flops=16 * length * size, bytes_accessed=8 * length * size, transcendentals=2 * length
        ),
    )(sources, gain[None, :], own, peer)


def after(value, earlier):
    return lax.optimization_barrier((value, earlier))[0]


def per_device(n_batch, n_hidden, tokens, segments, rel_bias, ln_gain, w_query, w_key, w_value, w_out):
    place = lax.axis_index("batch")
    column = lax.axis_index("hidden")
    parity = (place >> 1) & 1
    length, own_width = tokens.shape
    heads = rel_bias.shape[1] // 2
    half = w_query.shape[1] // 2
    width = half // heads

    def swap(value, step, axis="batch"):
        count = n_batch if axis == "batch" else n_hidden
        return lax.ppermute(value, axis, [(i, i ^ step) for i in range(count)])

    far = list(range(4, n_batch, 2))
    far_line, pair_line, near_line = [], [], []

    def paced(value, step, line, depth, *earlier):
        waits = tuple(line[-depth : len(line) - depth + 1]) + earlier
        if waits:
            value = after(value, waits)
        received = swap(value, step)
        line.append(received)
        return received

    def halves(weight, axis):
        size = weight.shape[axis] // 2
        return [
            lax.dynamic_slice_in_dim(weight, side * size, size, axis)
            for side in (parity, 1 - parity)
        ]

    def close_by(parts):
        return jnp.concatenate([parts[0], paced(parts[1], 2, pair_line, 1)], axis=0)

    def far_off(parts, *earlier):
        distant = {
            step: paced(parts[(step >> 1) & 1], step, far_line, 2, *earlier)
            for step in reversed(far)
        }
        return jnp.concatenate([distant[step] for step in far], axis=0)

    def gathered(close):
        planes = n_batch // 4
        size = close.shape[0]
        groups = [[r + 4 * i for i in range(planes)] for r in range(4)]
        whole = lax.all_gather(close, "batch", axis=0, tiled=True, axis_index_groups=groups)
        rest = [
            lax.dynamic_slice_in_dim(whole, ((place >> 2) ^ k) * size, size, 0)
            for k in range(1, planes)
        ]
        return rest[0] if len(rest) == 1 else jnp.concatenate(rest, axis=0)

    def along_x(value, *earlier):
        return paced(value, 1, near_line, 2, *earlier)

    peer_tokens = paced(tokens, 2, pair_line, 1)
    peer_ids = swap(segments, 2)
    own_all, peer_all = [
        lax.all_gather(part, "hidden", axis=1, tiled=True) for part in (tokens, peer_tokens)
    ]

    key_parts, query_parts = halves(w_key, 1), halves(w_query, 1)
    key_close = close_by(key_parts)
    key_far = far_off(key_parts)
    value_close = close_by(halves(w_value, 1))
    query_close = close_by(query_parts)
    query_far = far_off(query_parts, peer_all, value_close)
    out_close = close_by(halves(w_out, 0))

    key_near = along_x(key_close)
    query_near = along_x(query_close)
    value_far = gathered(after(value_close, (peer_all, far_line[0])))
    key_rest = along_x(key_far)
    value_near = along_x(value_close)
    query_rest = along_x(query_far)

    order = [0, 2] + far
    order += [step ^ 1 for step in order]
    normed = normalise(own_all, peer_all, ln_gain, jnp.stack([place ^ step for step in order]))

    table = lax.dynamic_slice_in_dim(rel_bias, parity * heads, heads, 1)
    bias = bias_tiles(table)

    def joined(values, axis):
        return values[0] if len(values) == 1 else jnp.concatenate(values, axis=axis)

    def project(*blocks):
        total, first = None, 0
        for rows in blocks:
            part = normed[:, first : first + rows.shape[0]]
            first += rows.shape[0]
            term = jnp.dot(part, rows, preferred_element_type=jnp.float32)
            total = term if total is None else total + term
        return total.astype(jnp.bfloat16)

    keys = project(key_close, key_far, key_near, key_rest)
    queries = project(query_close, query_far, query_near, query_rest)
    out_far = gathered(after(out_close, queries))
    out_near = along_x(out_close, normed)
    value_rest = along_x(value_far, normed)
    values = project(value_close, value_far, value_near, value_rest)
    out_rest = along_x(out_far, values)
    ids = jnp.concatenate([segments, peer_ids], axis=0)
    attended = attend(queries, keys, values, ids, bias, width)

    side = place & 1
    stripes = own_width // (2 * w_out.shape[1])

    def sums(rows):
        def block(step):
            first = (column ^ step) * stripes
            chosen = [
                lax.dynamic_slice_in_dim(rows, ((place >> 1) ^ (first + j)) * half, half, 0)
                for j in range(stripes)
            ]
            chosen = joined(chosen, 1)
            return jnp.dot(attended, chosen, preferred_element_type=jnp.float32)

        far = send(block(3), 1, "hidden")
        near = send(block(1), 1, "hidden")
        return block(0) + near, block(2) + far

    def send(value, step, axis="batch"):
        return swap(value.astype(jnp.bfloat16), step, axis).astype(jnp.float32)

    here, there = sums(jnp.concatenate([out_close, out_far], axis=0))
    received = send(there, 2, "hidden")
    first = here
    late = after(out_rest, (here, there))
    here, there = sums(jnp.concatenate([out_near, late], axis=0))
    there_peer = send(there[length:], 2)
    here_peer = send(here[length:], 2)
    first = first + after(received, (there_peer, here_peer))
    first = first[:length] + send(first[length:], 2)
    second = here[:length] + here_peer + send(there[:length] + there_peer, 2, "hidden")

    parts = [v.reshape(length, stripes, w_out.shape[1]) for v in (first, second)]
    combined = jnp.where(side == 0, jnp.stack(parts, 2), jnp.stack(parts[::-1], 2))
    return (tokens.astype(jnp.float32) + combined.reshape(length, own_width)).astype(jnp.bfloat16)


def solution(mesh):
    placed = (
        P("batch", "hidden"),
        P("batch", None),
        P(None, "hidden"),
        P(),
        P("batch", "hidden"),
        P("batch", "hidden"),
        P("batch", "hidden"),
        P("hidden", "batch"),
    )
    return jax.shard_map(
        functools.partial(per_device, mesh.shape["batch"], mesh.shape["hidden"]),
        mesh=mesh,
        in_specs=placed,
        out_specs=P("batch", "hidden"),
        check_vma=False,
    )
```

```python
import functools

import jax
import jax.numpy as jnp
from jax import lax
from jax.experimental import pallas as pl
from jax.experimental.pallas import tpu as pltpu
from jax.sharding import PartitionSpec as P

PASSAGE = 256
BLOCK = 128

norm_epsilon = 1e-06
bucket_edges = (12, 16, 23, 32, 46, 64, 91)
masked_score = -1e30


def bucket_of(offsets):
    distance = jnp.abs(offsets)
    reached = sum(((distance >= threshold).astype(jnp.int32) for threshold in bucket_edges))
    within = jnp.where(distance < 8, distance, 8 + reached)
    return within + jnp.where(offsets > 0, 16, 0)


def bias_tiles(table):
    rows = 2 * PASSAGE + BLOCK
    offsets = (
        jnp.arange(rows, dtype=jnp.int32)[:, None]
        - PASSAGE
        - jnp.arange(BLOCK, dtype=jnp.int32)[None, :]
    )
    buckets = bucket_of(offsets)[None]
    tiles = jnp.zeros((table.shape[1], rows, BLOCK), jnp.float32)
    for level in range(table.shape[0]):
        tiles = jnp.where(buckets == level, table[level][:, None, None], tiles)
    return tiles


def attention_kernel(width, q_ids, k_ids, bias, queries, keys, values, out):
    length = keys.shape[0]
    blocks = length // BLOCK
    reach = PASSAGE // BLOCK
    heads = keys.shape[1] // width
    turned = jnp.transpose(values[...].astype(jnp.float32)).astype(jnp.bfloat16)
    head_of = lax.broadcasted_iota(jnp.int32, (BLOCK, keys.shape[1]), 1) // width
    for i in range(blocks):
        low, high = max(0, i - reach) * BLOCK, min(blocks, i + reach + 1) * BLOCK
        columns = slice(i * BLOCK, (i + 1) * BLOCK)
        first = low - i * BLOCK + PASSAGE
        same = k_ids[low:high, :] == q_ids[:, columns]
        own = queries[columns, :]
        results = []
        for h in range(heads):
            chosen = jnp.where(head_of == h, own, jnp.zeros_like(own))
            scores = lax.dot_general(
                keys[low:high, :],
                chosen,
                (((1,), (1,)), ((), ())),
                preferred_element_type=jnp.float32,
            )
            scores = jnp.where(same, scores + bias[h, first : first + high - low, :], masked_score)
            raised = jnp.exp(scores - jnp.max(scores, axis=0, keepdims=True)).astype(jnp.bfloat16)
            extended = jnp.concatenate(
                [
                    turned[h * width : (h + 1) * width, low:high],
                    jnp.ones((16, high - low), jnp.bfloat16),
                ],
                axis=0,
            )
            total = jnp.dot(extended, raised, preferred_element_type=jnp.float32)
            results.append(total[:width] / total[width : width + 1])
        out[columns, :] = jnp.transpose(jnp.concatenate(results, axis=0)).astype(jnp.bfloat16)


def attend(queries, keys, values, ids, bias, width):
    groups, length = ids.shape
    features = keys.shape[1]
    heads = 128 // width
    wide_ids = jnp.broadcast_to(ids.reshape(-1)[:, None], (groups * length, BLOCK))
    block = pl.BlockSpec((length, 128), lambda g, p: (g, p))
    return pl.pallas_call(
        functools.partial(attention_kernel, width),
        grid=(groups, features // 128),
        in_specs=[
            pl.BlockSpec((None, 1, length), lambda g, p: (g, 0, 0)),
            pl.BlockSpec((length, BLOCK), lambda g, p: (g, 0)),
            pl.BlockSpec((heads,) + bias.shape[1:], lambda g, p: (p, 0, 0)),
            block,
            block,
            block,
        ],
        out_specs=block,
        out_shape=jax.ShapeDtypeStruct(queries.shape, jnp.bfloat16),
        compiler_params=pltpu.CompilerParams(vmem_limit_bytes=24 * 1024 * 1024),
        cost_estimate=pl.CostEstimate(
            flops=8 * groups * features * length * length,
            bytes_accessed=16 * groups * features * length,
            transcendentals=groups * features // width * length * length,
        ),
    )(ids[:, None, :], wide_ids, bias, queries, keys, values)


def normalise_kernel(sources, gain, own, peer, out):
    depth = out.shape[1] // sources.shape[0]
    for group, tokens in enumerate((own, peer)):

        @pl.when(pl.program_id(0) == group)
        def _():
            wide = tokens[...].astype(jnp.float32)
            scale = lax.rsqrt(jnp.mean(wide * wide, axis=1, keepdims=True) + norm_epsilon)
            for k in range(sources.shape[0]):
                start = pl.multiple_of(sources[k] * depth, 128)
                part = tokens[:, pl.ds(start, depth)].astype(jnp.float32)
                part = part * scale * gain[:, pl.ds(start, depth)]
                out[:, k * depth : (k + 1) * depth] = part.astype(jnp.bfloat16)


def normalise(own, peer, gain, sources):
    length, size = own.shape
    steps = length // BLOCK
    return pl.pallas_call(
        normalise_kernel,
        grid_spec=pltpu.PrefetchScalarGridSpec(
            num_scalar_prefetch=1,
            grid=(2, steps),
            in_specs=[
                pl.BlockSpec((1, size), lambda g, i, _: (0, 0)),
                pl.BlockSpec((BLOCK, size), lambda g, i, _: (jnp.where(g == 0, i, steps - 1), 0)),
                pl.BlockSpec((BLOCK, size), lambda g, i, _: (jnp.where(g == 0, 0, i), 0)),
            ],
            out_specs=pl.BlockSpec((BLOCK, size), lambda g, i, _: (g * steps + i, 0)),
        ),
        out_shape=jax.ShapeDtypeStruct((2 * length, size), jnp.bfloat16),
        compiler_params=pltpu.CompilerParams(vmem_limit_bytes=24 * 1024 * 1024),
        cost_estimate=pl.CostEstimate(
            flops=16 * length * size, bytes_accessed=8 * length * size, transcendentals=2 * length
        ),
    )(sources, gain[None, :], own, peer)


def after(value, earlier):
    return lax.optimization_barrier((value, earlier))[0]


def per_device(n_batch, n_hidden, tokens, segments, rel_bias, ln_gain, w_query, w_key, w_value, w_out):
    place = lax.axis_index("batch")
    column = lax.axis_index("hidden")
    parity = (place >> 1) & 1
    length, own_width = tokens.shape
    heads = rel_bias.shape[1] // 2
    half = w_query.shape[1] // 2
    width = half // heads

    def swap(value, step, axis="batch"):
        count = n_batch if axis == "batch" else n_hidden
        return lax.ppermute(value, axis, [(i, i ^ step) for i in range(count)])

    far = list(range(4, n_batch, 2))
    far_line, pair_line, near_line = [], [], []

    def paced(value, step, line, depth, *earlier):
        waits = tuple(line[-depth : len(line) - depth + 1]) + earlier
        if waits:
            value = after(value, waits)
        received = swap(value, step)
        line.append(received)
        return received

    def halves(weight, axis):
        size = weight.shape[axis] // 2
        return [
            lax.dynamic_slice_in_dim(weight, side * size, size, axis)
            for side in (parity, 1 - parity)
        ]

    def close_by(parts):
        return jnp.concatenate([parts[0], paced(parts[1], 2, pair_line, 1)], axis=0)

    def far_off(parts):
        distant = {
            step: paced(parts[(step >> 1) & 1], step, far_line, 2) for step in reversed(far)
        }
        return jnp.concatenate([distant[step] for step in far], axis=0)

    def gathered(close):
        planes = n_batch // 4
        size = close.shape[0]
        groups = [[r + 4 * i for i in range(planes)] for r in range(4)]
        whole = lax.all_gather(close, "batch", axis=0, tiled=True, axis_index_groups=groups)
        rest = [
            lax.dynamic_slice_in_dim(whole, ((place >> 2) ^ k) * size, size, 0)
            for k in range(1, planes)
        ]
        return rest[0] if len(rest) == 1 else jnp.concatenate(rest, axis=0)

    def along_x(value, *earlier):
        return paced(value, 1, near_line, 2, *earlier)

    peer_tokens = paced(tokens, 2, pair_line, 1)
    peer_ids = swap(segments, 2)
    own_all, peer_all = [
        lax.all_gather(part, "hidden", axis=1, tiled=True) for part in (tokens, peer_tokens)
    ]

    key_parts, query_parts = halves(w_key, 1), halves(w_query, 1)
    key_close = close_by(key_parts)
    key_far = far_off(key_parts)
    value_close = close_by(halves(w_value, 1))
    query_close = close_by(query_parts)
    query_far = far_off(query_parts)
    out_close = close_by(halves(w_out, 0))

    key_near = along_x(key_close)
    value_near = along_x(value_close)
    value_far = gathered(after(value_close, (own_all, far_line[0])))
    query_near = along_x(query_close)
    key_rest = along_x(key_far)
    query_rest = along_x(query_far)

    order = [0, 2] + far
    order += [step ^ 1 for step in order]
    normed = normalise(own_all, peer_all, ln_gain, jnp.stack([place ^ step for step in order]))

    table = lax.dynamic_slice_in_dim(rel_bias, parity * heads, heads, 1)
    bias = bias_tiles(table)

    def joined(values, axis):
        return values[0] if len(values) == 1 else jnp.concatenate(values, axis=axis)

    def project(*blocks):
        total, first = None, 0
        for rows in blocks:
            part = normed[:, first : first + rows.shape[0]]
            first += rows.shape[0]
            term = jnp.dot(part, rows, preferred_element_type=jnp.float32)
            total = term if total is None else total + term
        return total.astype(jnp.bfloat16)

    keys = project(key_close, key_far, key_near, key_rest)
    queries = project(query_close, query_far, query_near, query_rest)
    out_far = gathered(after(out_close, normed))
    out_near = along_x(out_close, normed)
    value_rest = along_x(value_far, normed)
    values = project(value_close, value_far, value_near, value_rest)
    out_rest = along_x(out_far, values)
    ids = jnp.concatenate([segments, peer_ids], axis=0)
    attended = attend(queries, keys, values, ids, bias, width)

    side = place & 1
    stripes = own_width // (2 * w_out.shape[1])

    def sums(rows):
        def block(step):
            first = (column ^ step) * stripes
            chosen = [
                lax.dynamic_slice_in_dim(rows, ((place >> 1) ^ (first + j)) * half, half, 0)
                for j in range(stripes)
            ]
            chosen = joined(chosen, 1)
            return jnp.dot(attended, chosen, preferred_element_type=jnp.float32)

        far = send(block(3), 1, "hidden")
        near = send(block(1), 1, "hidden")
        return block(0) + near, block(2) + far

    def send(value, step, axis="batch"):
        return swap(value.astype(jnp.bfloat16), step, axis).astype(jnp.float32)

    here, there = sums(jnp.concatenate([out_close, out_far], axis=0))
    received = send(there, 2, "hidden")
    first = here + received
    first = first[:length] + send(first[length:], 2)
    late = after(out_rest, (here, there))
    here, there = sums(jnp.concatenate([out_near, late], axis=0))
    both = send(jnp.concatenate([here[length:], there[length:]], axis=1), 2)
    middle = here.shape[1]
    there = there[:length] + both[:, middle:]
    second = here[:length] + both[:, :middle] + send(there, 2, "hidden")

    parts = [v.reshape(length, stripes, w_out.shape[1]) for v in (first, second)]
    combined = jnp.where(side == 0, jnp.stack(parts, 2), jnp.stack(parts[::-1], 2))
    return (tokens.astype(jnp.float32) + combined.reshape(length, own_width)).astype(jnp.bfloat16)


def solution(mesh):
    placed = (
        P("batch", "hidden"),
        P("batch", None),
        P(None, "hidden"),
        P(),
        P("batch", "hidden"),
        P("batch", "hidden"),
        P("batch", "hidden"),
        P("hidden", "batch"),
    )
    return jax.shard_map(
        functools.partial(per_device, mesh.shape["batch"], mesh.shape["hidden"]),
        mesh=mesh,
        in_specs=placed,
        out_specs=P("batch", "hidden"),
        check_vma=False,
    )
```

```python
import functools

import jax
import jax.numpy as jnp
from jax import lax
from jax.experimental import pallas as pl
from jax.experimental.pallas import tpu as pltpu
from jax.sharding import PartitionSpec as P

PASSAGE = 256
BLOCK = 128

norm_epsilon = 1e-06
bucket_edges = (12, 16, 23, 32, 46, 64, 91)
masked_score = -1e30


def bucket_of(offsets):
    distance = jnp.abs(offsets)
    reached = sum(((distance >= threshold).astype(jnp.int32) for threshold in bucket_edges))
    within = jnp.where(distance < 8, distance, 8 + reached)
    return within + jnp.where(offsets > 0, 16, 0)


def bias_tiles(table):
    rows = 2 * PASSAGE + BLOCK
    offsets = (
        jnp.arange(rows, dtype=jnp.int32)[:, None]
        - PASSAGE
        - jnp.arange(BLOCK, dtype=jnp.int32)[None, :]
    )
    buckets = bucket_of(offsets)[None]
    tiles = jnp.zeros((table.shape[1], rows, BLOCK), jnp.float32)
    for level in range(table.shape[0]):
        tiles = jnp.where(buckets == level, table[level][:, None, None], tiles)
    return tiles


def attention_kernel(width, q_ids, k_ids, bias, queries, keys, values, out):
    length = keys.shape[0]
    blocks = length // BLOCK
    reach = PASSAGE // BLOCK
    heads = keys.shape[1] // width
    turned = jnp.transpose(values[...].astype(jnp.float32)).astype(jnp.bfloat16)
    head_of = lax.broadcasted_iota(jnp.int32, (BLOCK, keys.shape[1]), 1) // width
    for i in range(blocks):
        low, high = max(0, i - reach) * BLOCK, min(blocks, i + reach + 1) * BLOCK
        columns = slice(i * BLOCK, (i + 1) * BLOCK)
        first = low - i * BLOCK + PASSAGE
        same = k_ids[low:high, :] == q_ids[:, columns]
        own = queries[columns, :]
        results = []
        for h in range(heads):
            chosen = jnp.where(head_of == h, own, jnp.zeros_like(own))
            scores = lax.dot_general(
                keys[low:high, :],
                chosen,
                (((1,), (1,)), ((), ())),
                preferred_element_type=jnp.float32,
            )
            scores = jnp.where(same, scores + bias[h, first : first + high - low, :], masked_score)
            raised = jnp.exp(scores - jnp.max(scores, axis=0, keepdims=True)).astype(jnp.bfloat16)
            extended = jnp.concatenate(
                [
                    turned[h * width : (h + 1) * width, low:high],
                    jnp.ones((16, high - low), jnp.bfloat16),
                ],
                axis=0,
            )
            total = jnp.dot(extended, raised, preferred_element_type=jnp.float32)
            results.append(total[:width] / total[width : width + 1])
        out[columns, :] = jnp.transpose(jnp.concatenate(results, axis=0)).astype(jnp.bfloat16)


def attend(queries, keys, values, ids, bias, width):
    groups, length = ids.shape
    features = keys.shape[1]
    heads = 128 // width
    wide_ids = jnp.broadcast_to(ids.reshape(-1)[:, None], (groups * length, BLOCK))
    block = pl.BlockSpec((length, 128), lambda g, p: (g, p))
    return pl.pallas_call(
        functools.partial(attention_kernel, width),
        grid=(groups, features // 128),
        in_specs=[
            pl.BlockSpec((None, 1, length), lambda g, p: (g, 0, 0)),
            pl.BlockSpec((length, BLOCK), lambda g, p: (g, 0)),
            pl.BlockSpec((heads,) + bias.shape[1:], lambda g, p: (p, 0, 0)),
            block,
            block,
            block,
        ],
        out_specs=block,
        out_shape=jax.ShapeDtypeStruct(queries.shape, jnp.bfloat16),
        compiler_params=pltpu.CompilerParams(vmem_limit_bytes=24 * 1024 * 1024),
        cost_estimate=pl.CostEstimate(
            flops=8 * groups * features * length * length,
            bytes_accessed=16 * groups * features * length,
            transcendentals=groups * features // width * length * length,
        ),
    )(ids[:, None, :], wide_ids, bias, queries, keys, values)


def normalise_kernel(sources, gain, own, peer, out):
    depth = out.shape[1] // sources.shape[0]
    for group, tokens in enumerate((own, peer)):

        @pl.when(pl.program_id(0) == group)
        def _():
            wide = tokens[...].astype(jnp.float32)
            scale = lax.rsqrt(jnp.mean(wide * wide, axis=1, keepdims=True) + norm_epsilon)
            for k in range(sources.shape[0]):
                start = pl.multiple_of(sources[k] * depth, 128)
                part = tokens[:, pl.ds(start, depth)].astype(jnp.float32)
                part = part * scale * gain[:, pl.ds(start, depth)]
                out[:, k * depth : (k + 1) * depth] = part.astype(jnp.bfloat16)


def normalise(own, peer, gain, sources):
    length, size = own.shape
    steps = length // BLOCK
    return pl.pallas_call(
        normalise_kernel,
        grid_spec=pltpu.PrefetchScalarGridSpec(
            num_scalar_prefetch=1,
            grid=(2, steps),
            in_specs=[
                pl.BlockSpec((1, size), lambda g, i, _: (0, 0)),
                pl.BlockSpec((BLOCK, size), lambda g, i, _: (jnp.where(g == 0, i, steps - 1), 0)),
                pl.BlockSpec((BLOCK, size), lambda g, i, _: (jnp.where(g == 0, 0, i), 0)),
            ],
            out_specs=pl.BlockSpec((BLOCK, size), lambda g, i, _: (g * steps + i, 0)),
        ),
        out_shape=jax.ShapeDtypeStruct((2 * length, size), jnp.bfloat16),
        compiler_params=pltpu.CompilerParams(vmem_limit_bytes=24 * 1024 * 1024),
        cost_estimate=pl.CostEstimate(
            flops=16 * length * size, bytes_accessed=8 * length * size, transcendentals=2 * length
        ),
    )(sources, gain[None, :], own, peer)


def after(value, earlier):
    return lax.optimization_barrier((value, earlier))[0]


def per_device(n_batch, n_hidden, tokens, segments, rel_bias, ln_gain, w_query, w_key, w_value, w_out):
    place = lax.axis_index("batch")
    column = lax.axis_index("hidden")
    parity = (place >> 1) & 1
    length, own_width = tokens.shape
    heads = rel_bias.shape[1] // 2
    half = w_query.shape[1] // 2
    width = half // heads

    def swap(value, step, axis="batch"):
        count = n_batch if axis == "batch" else n_hidden
        return lax.ppermute(value, axis, [(i, i ^ step) for i in range(count)])

    far = list(range(4, n_batch, 2))
    far_line, pair_line, near_line = [], [], []

    def paced(value, step, line, depth, *earlier):
        waits = tuple(line[-depth : len(line) - depth + 1]) + earlier
        if waits:
            value = after(value, waits)
        received = swap(value, step)
        line.append(received)
        return received

    def halves(weight, axis):
        size = weight.shape[axis] // 2
        return [
            lax.dynamic_slice_in_dim(weight, side * size, size, axis)
            for side in (parity, 1 - parity)
        ]

    def close_by(parts):
        return jnp.concatenate([parts[0], paced(parts[1], 2, pair_line, 1)], axis=0)

    def far_off(parts):
        distant = {
            step: paced(parts[(step >> 1) & 1], step, far_line, 2) for step in reversed(far)
        }
        return jnp.concatenate([distant[step] for step in far], axis=0)

    def gathered(close):
        planes = n_batch // 4
        size = close.shape[0]
        groups = [[r + 4 * i for i in range(planes)] for r in range(4)]
        whole = lax.all_gather(close, "batch", axis=0, tiled=True, axis_index_groups=groups)
        rest = [
            lax.dynamic_slice_in_dim(whole, ((place >> 2) ^ k) * size, size, 0)
            for k in range(1, planes)
        ]
        return rest[0] if len(rest) == 1 else jnp.concatenate(rest, axis=0)

    def along_x(value, *earlier):
        return paced(value, 1, near_line, 2, *earlier)

    key_parts, query_parts = halves(w_key, 1), halves(w_query, 1)
    value_close = close_by(halves(w_value, 1))
    key_far = far_off(key_parts)

    peer_tokens = paced(tokens, 2, pair_line, 1, far_line[0])
    peer_ids = swap(segments, 2)
    own_all, peer_all = [
        lax.all_gather(part, "hidden", axis=1, tiled=True) for part in (tokens, peer_tokens)
    ]

    key_close = close_by(key_parts)
    query_close = close_by(query_parts)
    query_far = far_off(query_parts)
    out_close = close_by(halves(w_out, 0))

    value_near = along_x(value_close)
    key_near = along_x(key_close)
    value_far = gathered(after(value_close, own_all))
    query_near = along_x(query_close)
    key_rest = along_x(key_far)
    query_rest = along_x(query_far)

    order = [0, 2] + far
    order += [step ^ 1 for step in order]
    normed = normalise(own_all, peer_all, ln_gain, jnp.stack([place ^ step for step in order]))

    table = lax.dynamic_slice_in_dim(rel_bias, parity * heads, heads, 1)
    bias = bias_tiles(table)

    def joined(values, axis):
        return values[0] if len(values) == 1 else jnp.concatenate(values, axis=axis)

    def project(*blocks):
        total, first = None, 0
        for rows in blocks:
            part = normed[:, first : first + rows.shape[0]]
            first += rows.shape[0]
            term = jnp.dot(part, rows, preferred_element_type=jnp.float32)
            total = term if total is None else total + term
        return total.astype(jnp.bfloat16)

    keys = project(key_close, key_far, key_near, key_rest)
    queries = project(query_close, query_far, query_near, query_rest)
    out_far = gathered(after(out_close, normed))
    out_near = along_x(out_close, normed)
    value_rest = along_x(value_far, normed)
    values = project(value_close, value_far, value_near, value_rest)
    out_rest = along_x(out_far, values)
    ids = jnp.concatenate([segments, peer_ids], axis=0)
    attended = attend(queries, keys, values, ids, bias, width)

    side = place & 1
    stripes = own_width // (2 * w_out.shape[1])

    def sums(rows):
        def block(step):
            first = (column ^ step) * stripes
            chosen = [
                lax.dynamic_slice_in_dim(rows, ((place >> 1) ^ (first + j)) * half, half, 0)
                for j in range(stripes)
            ]
            chosen = joined(chosen, 1)
            return jnp.dot(attended, chosen, preferred_element_type=jnp.float32)

        far = send(block(3), 1, "hidden")
        near = send(block(1), 1, "hidden")
        return block(0) + near, block(2) + far

    def send(value, step, axis="batch"):
        return swap(value.astype(jnp.bfloat16), step, axis).astype(jnp.float32)

    here, there = sums(jnp.concatenate([out_close, out_far], axis=0))
    received = send(there, 2, "hidden")
    first = here + received
    first = first[:length] + send(first[length:], 2)
    late = after(out_rest, (here, there))
    here, there = sums(jnp.concatenate([out_near, late], axis=0))
    both = send(jnp.concatenate([here[length:], there[length:]], axis=1), 2)
    middle = here.shape[1]
    there = there[:length] + both[:, middle:]
    second = here[:length] + both[:, :middle] + send(there, 2, "hidden")

    parts = [v.reshape(length, stripes, w_out.shape[1]) for v in (first, second)]
    combined = jnp.where(side == 0, jnp.stack(parts, 2), jnp.stack(parts[::-1], 2))
    return (tokens.astype(jnp.float32) + combined.reshape(length, own_width)).astype(jnp.bfloat16)


def solution(mesh):
    placed = (
        P("batch", "hidden"),
        P("batch", None),
        P(None, "hidden"),
        P(),
        P("batch", "hidden"),
        P("batch", "hidden"),
        P("batch", "hidden"),
        P("hidden", "batch"),
    )
    return jax.shard_map(
        functools.partial(per_device, mesh.shape["batch"], mesh.shape["hidden"]),
        mesh=mesh,
        in_specs=placed,
        out_specs=P("batch", "hidden"),
        check_vma=False,
    )
```

```python
import functools

import jax
import jax.numpy as jnp
from jax import lax
from jax.experimental import pallas as pl
from jax.experimental.pallas import tpu as pltpu
from jax.sharding import PartitionSpec as P

PASSAGE = 256
BLOCK = 128

norm_epsilon = 1e-06
bucket_edges = (12, 16, 23, 32, 46, 64, 91)
masked_score = -1e30


def bucket_of(offsets):
    distance = jnp.abs(offsets)
    reached = sum(((distance >= threshold).astype(jnp.int32) for threshold in bucket_edges))
    within = jnp.where(distance < 8, distance, 8 + reached)
    return within + jnp.where(offsets > 0, 16, 0)


def bias_tiles(table):
    rows = 2 * PASSAGE + BLOCK
    offsets = (
        jnp.arange(rows, dtype=jnp.int32)[:, None]
        - PASSAGE
        - jnp.arange(BLOCK, dtype=jnp.int32)[None, :]
    )
    buckets = bucket_of(offsets)[None]
    tiles = jnp.zeros((table.shape[1], rows, BLOCK), jnp.float32)
    for level in range(table.shape[0]):
        tiles = jnp.where(buckets == level, table[level][:, None, None], tiles)
    return tiles


def attention_kernel(width, q_ids, k_ids, bias, queries, keys, values, out):
    length = keys.shape[0]
    blocks = length // BLOCK
    reach = PASSAGE // BLOCK
    heads = keys.shape[1] // width
    turned = jnp.transpose(values[...].astype(jnp.float32)).astype(jnp.bfloat16)
    head_of = lax.broadcasted_iota(jnp.int32, (BLOCK, keys.shape[1]), 1) // width
    for i in range(blocks):
        low, high = max(0, i - reach) * BLOCK, min(blocks, i + reach + 1) * BLOCK
        columns = slice(i * BLOCK, (i + 1) * BLOCK)
        first = low - i * BLOCK + PASSAGE
        same = k_ids[low:high, :] == q_ids[:, columns]
        own = queries[columns, :]
        results = []
        for h in range(heads):
            chosen = jnp.where(head_of == h, own, jnp.zeros_like(own))
            scores = lax.dot_general(
                keys[low:high, :],
                chosen,
                (((1,), (1,)), ((), ())),
                preferred_element_type=jnp.float32,
            )
            scores = jnp.where(same, scores + bias[h, first : first + high - low, :], masked_score)
            raised = jnp.exp(scores - jnp.max(scores, axis=0, keepdims=True)).astype(jnp.bfloat16)
            extended = jnp.concatenate(
                [
                    turned[h * width : (h + 1) * width, low:high],
                    jnp.ones((16, high - low), jnp.bfloat16),
                ],
                axis=0,
            )
            total = jnp.dot(extended, raised, preferred_element_type=jnp.float32)
            results.append(total[:width] / total[width : width + 1])
        out[columns, :] = jnp.transpose(jnp.concatenate(results, axis=0)).astype(jnp.bfloat16)


def attend(queries, keys, values, ids, bias, width):
    groups, length = ids.shape
    features = keys.shape[1]
    heads = 128 // width
    wide_ids = jnp.broadcast_to(ids.reshape(-1)[:, None], (groups * length, BLOCK))
    block = pl.BlockSpec((length, 128), lambda g, p: (g, p))
    return pl.pallas_call(
        functools.partial(attention_kernel, width),
        grid=(groups, features // 128),
        in_specs=[
            pl.BlockSpec((None, 1, length), lambda g, p: (g, 0, 0)),
            pl.BlockSpec((length, BLOCK), lambda g, p: (g, 0)),
            pl.BlockSpec((heads,) + bias.shape[1:], lambda g, p: (p, 0, 0)),
            block,
            block,
            block,
        ],
        out_specs=block,
        out_shape=jax.ShapeDtypeStruct(queries.shape, jnp.bfloat16),
        compiler_params=pltpu.CompilerParams(vmem_limit_bytes=24 * 1024 * 1024),
        cost_estimate=pl.CostEstimate(
            flops=8 * groups * features * length * length,
            bytes_accessed=16 * groups * features * length,
            transcendentals=groups * features // width * length * length,
        ),
    )(ids[:, None, :], wide_ids, bias, queries, keys, values)


def normalise_kernel(sources, gain, own, peer, out):
    depth = out.shape[1] // sources.shape[0]
    for group, tokens in enumerate((own, peer)):

        @pl.when(pl.program_id(0) == group)
        def _():
            wide = tokens[...].astype(jnp.float32)
            scale = lax.rsqrt(jnp.mean(wide * wide, axis=1, keepdims=True) + norm_epsilon)
            for k in range(sources.shape[0]):
                start = pl.multiple_of(sources[k] * depth, 128)
                part = tokens[:, pl.ds(start, depth)].astype(jnp.float32)
                part = part * scale * gain[:, pl.ds(start, depth)]
                out[:, k * depth : (k + 1) * depth] = part.astype(jnp.bfloat16)


def normalise(own, peer, gain, sources):
    length, size = own.shape
    steps = length // BLOCK
    return pl.pallas_call(
        normalise_kernel,
        grid_spec=pltpu.PrefetchScalarGridSpec(
            num_scalar_prefetch=1,
            grid=(2, steps),
            in_specs=[
                pl.BlockSpec((1, size), lambda g, i, _: (0, 0)),
                pl.BlockSpec((BLOCK, size), lambda g, i, _: (jnp.where(g == 0, i, steps - 1), 0)),
                pl.BlockSpec((BLOCK, size), lambda g, i, _: (jnp.where(g == 0, 0, i), 0)),
            ],
            out_specs=pl.BlockSpec((BLOCK, size), lambda g, i, _: (g * steps + i, 0)),
        ),
        out_shape=jax.ShapeDtypeStruct((2 * length, size), jnp.bfloat16),
        compiler_params=pltpu.CompilerParams(vmem_limit_bytes=24 * 1024 * 1024),
        cost_estimate=pl.CostEstimate(
            flops=16 * length * size, bytes_accessed=8 * length * size, transcendentals=2 * length
        ),
    )(sources, gain[None, :], own, peer)


def after(value, earlier):
    return lax.optimization_barrier((value, earlier))[0]


def per_device(n_batch, n_hidden, tokens, segments, rel_bias, ln_gain, w_query, w_key, w_value, w_out):
    place = lax.axis_index("batch")
    column = lax.axis_index("hidden")
    parity = (place >> 1) & 1
    length, own_width = tokens.shape
    heads = rel_bias.shape[1] // 2
    half = w_query.shape[1] // 2
    width = half // heads

    def swap(value, step, axis="batch"):
        count = n_batch if axis == "batch" else n_hidden
        return lax.ppermute(value, axis, [(i, i ^ step) for i in range(count)])

    far = list(range(4, n_batch, 2))
    far_line, pair_line, near_line = [], [], []

    def paced(value, step, line, depth, *earlier):
        waits = tuple(line[-depth : len(line) - depth + 1]) + earlier
        if waits:
            value = after(value, waits)
        received = swap(value, step)
        line.append(received)
        return received

    def halves(weight, axis):
        size = weight.shape[axis] // 2
        return [
            lax.dynamic_slice_in_dim(weight, side * size, size, axis)
            for side in (parity, 1 - parity)
        ]

    def close_by(parts):
        return jnp.concatenate([parts[0], paced(parts[1], 2, pair_line, 1)], axis=0)

    def far_off(parts):
        distant = {
            step: paced(parts[(step >> 1) & 1], step, far_line, 2) for step in reversed(far)
        }
        return jnp.concatenate([distant[step] for step in far], axis=0)

    def gathered(close):
        planes = n_batch // 4
        size = close.shape[0]
        groups = [[r + 4 * i for i in range(planes)] for r in range(4)]
        whole = lax.all_gather(close, "batch", axis=0, tiled=True, axis_index_groups=groups)
        rest = [
            lax.dynamic_slice_in_dim(whole, ((place >> 2) ^ k) * size, size, 0)
            for k in range(1, planes)
        ]
        return rest[0] if len(rest) == 1 else jnp.concatenate(rest, axis=0)

    def along_x(value, *earlier):
        return paced(value, 1, near_line, 2, *earlier)

    key_parts, query_parts = halves(w_key, 1), halves(w_query, 1)
    value_close = close_by(halves(w_value, 1))
    key_far = far_off(key_parts)

    peer_tokens = paced(tokens, 2, pair_line, 1, far_line[0])
    peer_ids = swap(segments, 2)
    own_all = lax.all_gather(tokens, "hidden", axis=1, tiled=True)
    value_far = gathered(after(value_close, own_all))
    peer_all = lax.all_gather(after(peer_tokens, (value_far, far_line[1])), "hidden", axis=1, tiled=True)

    key_close = close_by(key_parts)
    query_close = close_by(query_parts)
    query_far = far_off(query_parts)
    out_close = close_by(halves(w_out, 0))

    value_near = along_x(value_close)
    key_near = along_x(key_close)
    query_near = along_x(query_close)
    key_rest = along_x(key_far)
    query_rest = along_x(query_far)

    order = [0, 2] + far
    order += [step ^ 1 for step in order]
    normed = normalise(own_all, peer_all, ln_gain, jnp.stack([place ^ step for step in order]))

    table = lax.dynamic_slice_in_dim(rel_bias, parity * heads, heads, 1)
    bias = bias_tiles(table)

    def joined(values, axis):
        return values[0] if len(values) == 1 else jnp.concatenate(values, axis=axis)

    def project(*blocks):
        total, first = None, 0
        for rows in blocks:
            part = normed[:, first : first + rows.shape[0]]
            first += rows.shape[0]
            term = jnp.dot(part, rows, preferred_element_type=jnp.float32)
            total = term if total is None else total + term
        return total.astype(jnp.bfloat16)

    keys = project(key_close, key_far, key_near, key_rest)
    queries = project(query_close, query_far, query_near, query_rest)
    out_far = gathered(after(out_close, normed))
    out_near = along_x(out_close, normed)
    value_rest = along_x(value_far)
    values = project(value_close, value_far, value_near, value_rest)
    out_rest = along_x(out_far, values)
    ids = jnp.concatenate([segments, peer_ids], axis=0)
    attended = attend(queries, keys, values, ids, bias, width)

    side = place & 1
    stripes = own_width // (2 * w_out.shape[1])

    def sums(rows):
        def block(step):
            first = (column ^ step) * stripes
            chosen = [
                lax.dynamic_slice_in_dim(rows, ((place >> 1) ^ (first + j)) * half, half, 0)
                for j in range(stripes)
            ]
            chosen = joined(chosen, 1)
            return jnp.dot(attended, chosen, preferred_element_type=jnp.float32)

        far = send(block(3), 1, "hidden")
        near = send(block(1), 1, "hidden")
        return block(0) + near, block(2) + far

    def send(value, step, axis="batch"):
        return swap(value.astype(jnp.bfloat16), step, axis).astype(jnp.float32)

    here, there = sums(jnp.concatenate([out_close, out_far], axis=0))
    received = send(there, 2, "hidden")
    first = here + received
    first = first[:length] + send(first[length:], 2)
    late = after(out_rest, (here, there))
    here, there = sums(jnp.concatenate([out_near, late], axis=0))
    both = send(jnp.concatenate([here[length:], there[length:]], axis=1), 2)
    middle = here.shape[1]
    there = there[:length] + both[:, middle:]
    second = here[:length] + both[:, :middle] + send(there, 2, "hidden")

    parts = [v.reshape(length, stripes, w_out.shape[1]) for v in (first, second)]
    combined = jnp.where(side == 0, jnp.stack(parts, 2), jnp.stack(parts[::-1], 2))
    return (tokens.astype(jnp.float32) + combined.reshape(length, own_width)).astype(jnp.bfloat16)


def solution(mesh):
    placed = (
        P("batch", "hidden"),
        P("batch", None),
        P(None, "hidden"),
        P(),
        P("batch", "hidden"),
        P("batch", "hidden"),
        P("batch", "hidden"),
        P("hidden", "batch"),
    )
    return jax.shard_map(
        functools.partial(per_device, mesh.shape["batch"], mesh.shape["hidden"]),
        mesh=mesh,
        in_specs=placed,
        out_specs=P("batch", "hidden"),
        check_vma=False,
    )
```

```python
import functools

import jax
import jax.numpy as jnp
from jax import lax
from jax.experimental import pallas as pl
from jax.experimental.pallas import tpu as pltpu
from jax.sharding import PartitionSpec as P

PASSAGE = 256
BLOCK = 128

norm_epsilon = 1e-06
bucket_edges = (12, 16, 23, 32, 46, 64, 91)
masked_score = -1e30


def bucket_of(offsets):
    distance = jnp.abs(offsets)
    reached = sum(((distance >= threshold).astype(jnp.int32) for threshold in bucket_edges))
    within = jnp.where(distance < 8, distance, 8 + reached)
    return within + jnp.where(offsets > 0, 16, 0)


def bias_tiles(table):
    rows = 2 * PASSAGE + BLOCK
    offsets = (
        jnp.arange(rows, dtype=jnp.int32)[:, None]
        - PASSAGE
        - jnp.arange(BLOCK, dtype=jnp.int32)[None, :]
    )
    buckets = bucket_of(offsets)[None]
    tiles = jnp.zeros((table.shape[1], rows, BLOCK), jnp.float32)
    for level in range(table.shape[0]):
        tiles = jnp.where(buckets == level, table[level][:, None, None], tiles)
    return tiles


def attention_kernel(width, q_ids, k_ids, bias, queries, keys, values, out):
    length = keys.shape[0]
    blocks = length // BLOCK
    reach = PASSAGE // BLOCK
    heads = keys.shape[1] // width
    turned = jnp.transpose(values[...].astype(jnp.float32)).astype(jnp.bfloat16)
    head_of = lax.broadcasted_iota(jnp.int32, (BLOCK, keys.shape[1]), 1) // width
    for i in range(blocks):
        low, high = max(0, i - reach) * BLOCK, min(blocks, i + reach + 1) * BLOCK
        columns = slice(i * BLOCK, (i + 1) * BLOCK)
        first = low - i * BLOCK + PASSAGE
        same = k_ids[low:high, :] == q_ids[:, columns]
        own = queries[columns, :]
        results = []
        for h in range(heads):
            chosen = jnp.where(head_of == h, own, jnp.zeros_like(own))
            scores = lax.dot_general(
                keys[low:high, :],
                chosen,
                (((1,), (1,)), ((), ())),
                preferred_element_type=jnp.float32,
            )
            scores = jnp.where(same, scores + bias[h, first : first + high - low, :], masked_score)
            raised = jnp.exp(scores - jnp.max(scores, axis=0, keepdims=True)).astype(jnp.bfloat16)
            extended = jnp.concatenate(
                [
                    turned[h * width : (h + 1) * width, low:high],
                    jnp.ones((16, high - low), jnp.bfloat16),
                ],
                axis=0,
            )
            total = jnp.dot(extended, raised, preferred_element_type=jnp.float32)
            results.append(total[:width] / total[width : width + 1])
        out[columns, :] = jnp.transpose(jnp.concatenate(results, axis=0)).astype(jnp.bfloat16)


def attend(queries, keys, values, ids, bias, width):
    groups, length = ids.shape
    features = keys.shape[1]
    heads = 128 // width
    wide_ids = jnp.broadcast_to(ids.reshape(-1)[:, None], (groups * length, BLOCK))
    block = pl.BlockSpec((length, 128), lambda g, p: (g, p))
    return pl.pallas_call(
        functools.partial(attention_kernel, width),
        grid=(groups, features // 128),
        in_specs=[
            pl.BlockSpec((None, 1, length), lambda g, p: (g, 0, 0)),
            pl.BlockSpec((length, BLOCK), lambda g, p: (g, 0)),
            pl.BlockSpec((heads,) + bias.shape[1:], lambda g, p: (p, 0, 0)),
            block,
            block,
            block,
        ],
        out_specs=block,
        out_shape=jax.ShapeDtypeStruct(queries.shape, jnp.bfloat16),
        compiler_params=pltpu.CompilerParams(vmem_limit_bytes=24 * 1024 * 1024),
        cost_estimate=pl.CostEstimate(
            flops=8 * groups * features * length * length,
            bytes_accessed=16 * groups * features * length,
            transcendentals=groups * features // width * length * length,
        ),
    )(ids[:, None, :], wide_ids, bias, queries, keys, values)


def normalise_kernel(sources, gain, own, peer, out):
    depth = out.shape[1] // sources.shape[0]
    for group, tokens in enumerate((own, peer)):

        @pl.when(pl.program_id(0) == group)
        def _():
            wide = tokens[...].astype(jnp.float32)
            scale = lax.rsqrt(jnp.mean(wide * wide, axis=1, keepdims=True) + norm_epsilon)
            for k in range(sources.shape[0]):
                start = pl.multiple_of(sources[k] * depth, 128)
                part = tokens[:, pl.ds(start, depth)].astype(jnp.float32)
                part = part * scale * gain[:, pl.ds(start, depth)]
                out[:, k * depth : (k + 1) * depth] = part.astype(jnp.bfloat16)


def normalise(own, peer, gain, sources):
    length, size = own.shape
    steps = length // BLOCK
    return pl.pallas_call(
        normalise_kernel,
        grid_spec=pltpu.PrefetchScalarGridSpec(
            num_scalar_prefetch=1,
            grid=(2, steps),
            in_specs=[
                pl.BlockSpec((1, size), lambda g, i, _: (0, 0)),
                pl.BlockSpec((BLOCK, size), lambda g, i, _: (jnp.where(g == 0, i, steps - 1), 0)),
                pl.BlockSpec((BLOCK, size), lambda g, i, _: (jnp.where(g == 0, 0, i), 0)),
            ],
            out_specs=pl.BlockSpec((BLOCK, size), lambda g, i, _: (g * steps + i, 0)),
        ),
        out_shape=jax.ShapeDtypeStruct((2 * length, size), jnp.bfloat16),
        compiler_params=pltpu.CompilerParams(vmem_limit_bytes=24 * 1024 * 1024),
        cost_estimate=pl.CostEstimate(
            flops=16 * length * size, bytes_accessed=8 * length * size, transcendentals=2 * length
        ),
    )(sources, gain[None, :], own, peer)


def after(value, earlier):
    return lax.optimization_barrier((value, earlier))[0]


def per_device(n_batch, n_hidden, tokens, segments, rel_bias, ln_gain, w_query, w_key, w_value, w_out):
    place = lax.axis_index("batch")
    column = lax.axis_index("hidden")
    parity = (place >> 1) & 1
    length, own_width = tokens.shape
    heads = rel_bias.shape[1] // 2
    half = w_query.shape[1] // 2
    width = half // heads

    def swap(value, step, axis="batch"):
        count = n_batch if axis == "batch" else n_hidden
        return lax.ppermute(value, axis, [(i, i ^ step) for i in range(count)])

    far = list(range(4, n_batch, 2))
    far_line, pair_line, near_line = [], [], []

    def paced(value, step, line, depth, *earlier):
        waits = tuple(line[-depth : len(line) - depth + 1]) + earlier
        if waits:
            value = after(value, waits)
        received = swap(value, step)
        line.append(received)
        return received

    def halves(weight, axis):
        size = weight.shape[axis] // 2
        return [
            lax.dynamic_slice_in_dim(weight, side * size, size, axis)
            for side in (parity, 1 - parity)
        ]

    def close_by(parts, *earlier):
        return jnp.concatenate([parts[0], paced(parts[1], 2, pair_line, 1, *earlier)], axis=0)

    def far_off(parts):
        distant = {
            step: paced(parts[(step >> 1) & 1], step, far_line, 2) for step in reversed(far)
        }
        return jnp.concatenate([distant[step] for step in far], axis=0)

    def gathered(close):
        planes = n_batch // 4
        size = close.shape[0]
        groups = [[r + 4 * i for i in range(planes)] for r in range(4)]
        whole = lax.all_gather(close, "batch", axis=0, tiled=True, axis_index_groups=groups)
        rest = [
            lax.dynamic_slice_in_dim(whole, ((place >> 2) ^ k) * size, size, 0)
            for k in range(1, planes)
        ]
        return rest[0] if len(rest) == 1 else jnp.concatenate(rest, axis=0)

    def along_x(value, *earlier):
        return paced(value, 1, near_line, 2, *earlier)

    key_parts, query_parts = halves(w_key, 1), halves(w_query, 1)
    value_close = close_by(halves(w_value, 1))
    key_far = far_off(key_parts)

    peer_tokens = paced(tokens, 2, pair_line, 1, far_line[0])
    peer_ids = swap(segments, 2)
    own_all, peer_all = [
        lax.all_gather(part, "hidden", axis=1, tiled=True) for part in (tokens, peer_tokens)
    ]

    key_close = close_by(key_parts, value_close)
    query_close = close_by(query_parts)
    query_far = far_off(query_parts)
    out_close = close_by(halves(w_out, 0))

    value_near = along_x(value_close)
    key_near = along_x(key_close)
    value_far = gathered(after(value_close, own_all))
    query_near = along_x(query_close)
    key_rest = along_x(key_far)
    query_rest = along_x(query_far)

    order = [0, 2] + far
    order += [step ^ 1 for step in order]
    normed = normalise(own_all, peer_all, ln_gain, jnp.stack([place ^ step for step in order]))

    table = lax.dynamic_slice_in_dim(rel_bias, parity * heads, heads, 1)
    bias = bias_tiles(table)

    def joined(values, axis):
        return values[0] if len(values) == 1 else jnp.concatenate(values, axis=axis)

    def project(*blocks):
        total, first = None, 0
        for rows in blocks:
            part = normed[:, first : first + rows.shape[0]]
            first += rows.shape[0]
            term = jnp.dot(part, rows, preferred_element_type=jnp.float32)
            total = term if total is None else total + term
        return total.astype(jnp.bfloat16)

    keys = project(key_close, key_far, key_near, key_rest)
    queries = project(query_close, query_far, query_near, query_rest)
    out_far = gathered(after(out_close, normed))
    out_near = along_x(out_close, normed)
    value_rest = along_x(value_far, normed)
    values = project(value_close, value_far, value_near, value_rest)
    out_rest = along_x(out_far, values)
    ids = jnp.concatenate([segments, peer_ids], axis=0)
    attended = attend(queries, keys, values, ids, bias, width)

    side = place & 1
    stripes = own_width // (2 * w_out.shape[1])

    def sums(rows):
        def block(step):
            first = (column ^ step) * stripes
            chosen = [
                lax.dynamic_slice_in_dim(rows, ((place >> 1) ^ (first + j)) * half, half, 0)
                for j in range(stripes)
            ]
            chosen = joined(chosen, 1)
            return jnp.dot(attended, chosen, preferred_element_type=jnp.float32)

        far = send(block(3), 1, "hidden")
        near = send(block(1), 1, "hidden")
        return block(0) + near, block(2) + far

    def send(value, step, axis="batch"):
        return swap(value.astype(jnp.bfloat16), step, axis).astype(jnp.float32)

    here, there = sums(jnp.concatenate([out_close, out_far], axis=0))
    received = send(there, 2, "hidden")
    first = here + received
    first = first[:length] + send(first[length:], 2)
    late = after(out_rest, (here, there))
    here, there = sums(jnp.concatenate([out_near, late], axis=0))
    both = send(jnp.concatenate([here[length:], there[length:]], axis=1), 2)
    middle = here.shape[1]
    there = there[:length] + both[:, middle:]
    second = here[:length] + both[:, :middle] + send(there, 2, "hidden")

    parts = [v.reshape(length, stripes, w_out.shape[1]) for v in (first, second)]
    combined = jnp.where(side == 0, jnp.stack(parts, 2), jnp.stack(parts[::-1], 2))
    return (tokens.astype(jnp.float32) + combined.reshape(length, own_width)).astype(jnp.bfloat16)


def solution(mesh):
    placed = (
        P("batch", "hidden"),
        P("batch", None),
        P(None, "hidden"),
        P(),
        P("batch", "hidden"),
        P("batch", "hidden"),
        P("batch", "hidden"),
        P("hidden", "batch"),
    )
    return jax.shard_map(
        functools.partial(per_device, mesh.shape["batch"], mesh.shape["hidden"]),
        mesh=mesh,
        in_specs=placed,
        out_specs=P("batch", "hidden"),
        check_vma=False,
    )
```
